32 devices in a mesh: groups: 2 (over y), dp: 4 (over z), mp: 2 (over x), teach: 2 (over core).
Axes of the slice: x: 2, y: 2, z: 4, core: 2. Of those that a mesh axis runs over, the one named last changes fastest.
Arguments:
- resid: bfloat16 [16, 256, 1280], P(('groups', 'dp', 'teach')), parts along dimension 0, may hold values from -6 to 6
- gain_mlp: float32 [1280], replicated, may hold values from 0.25 to 1.75
- gain_out: float32 [1280], replicated, may hold values from 0.25 to 1.75
- w_in: bfloat16 [1280, 5120], P(None, 'mp'), may hold values from -0.15625 to 0.15625
- w_out: bfloat16 [5120, 1280], P('mp'), may hold values from -0.078125 to 0.078125
- a_dino: bfloat16 [1280, 1536], P(None, 'mp'), may hold values from -0.15625 to 0.15625
- b_dino: bfloat16 [1536, 1536], P('mp')
- a_sig: bfloat16 [1280, 1152], P(None, 'mp'), may hold values from -0.15625 to 0.15625
- b_sig: bfloat16 [1152, 1152], P('mp')
- dino_feats: bfloat16 [16, 256, 1536], P('groups', ('dp', 'teach'), 'mp'), parts along dimension 0
- sig_feats: bfloat16 [16, 256, 1152], P('groups', ('dp', 'teach'), 'mp'), parts along dimension 0
- owner: int32 [16], P('groups'), parts along dimension 0, may hold values from 0 to 7, each once
Outputs:
- grad_w_in: float32 [2560, 5120], P(('groups', 'dp', 'teach'), 'mp'), parts along dimension 0
- grad_w_out: float32 [10240, 1280], P(('groups', 'mp'), ('dp', 'teach')), parts along dimension 0
- grad_a_dino: float32 [2560, 1536], P(('groups', 'dp', 'teach'), 'mp'), parts along dimension 0
- grad_b_dino: float32 [3072, 1536], P(('groups', 'mp'), ('dp', 'teach')), parts along dimension 0
- grad_a_sig: float32 [2560, 1152], P(('groups', 'dp', 'teach'), 'mp'), parts along dimension 0
- grad_b_sig: float32 [2304, 1152], P(('groups', 'mp'), ('dp', 'teach')), parts along dimension 0
The draws below stay inside these ranges and needn't reach their ends.
There are 2 independent parts, one for each index of `groups`. The reference program is written for one: setup_inputs(seed, part) draws one part's arguments, and reference() takes and returns one part's arrays. A program takes and returns all parts, laid end to end along the dimension named above; an argument that names none is the same for every part. Nothing has to cross between parts.
Inputs may be any that keep to these rules, and one draw needn't show every extreme that they name: owner is a permutation of the images of a group.
All inputs are finite; a program needn't handle non-finite values.
Results may differ from the reference program's by a relative error of at most 0.022.
Values may be sent and summed in bfloat16 or wider, within the bound.
No kernel may reach another device: no remote copies, remote signals or barrier semaphores. Data moves between devices by JAX's collectives and lax.ppermute only.
A program may use at most 128 MiB of HBM per device.

```python
import math
import jax
import jax.numpy as jnp
from jax import lax

D = 1280
FF = 5120
DD = 1536
DS = 1152
P_SIZE = 256
IMG_DEV = 1
IMAGES = 8
N_DP = 4
N_TEACH = 2


def column_scales(key, count):
    ramp = 0.5 + jnp.arange(count, dtype=jnp.float32) / count
    spread = jnp.exp(jax.random.uniform(key, (count,), jnp.float32, -1.15, 1.15))
    return ramp * spread


def draw_b_dino(key, part):
    key = jax.random.fold_in(key, 5)
    first, second = jax.random.split(key)
    base = jax.random.normal(first, (DD, DD), jnp.float32)
    return (base * column_scales(second, DD) / (1.5 * math.sqrt(DD))).astype(jnp.bfloat16)


def draw_b_sig(key, part):
    key = jax.random.fold_in(key, 6)
    first, second = jax.random.split(key)
    base = jax.random.normal(first, (DS, DS), jnp.float32)
    return (base * column_scales(second, DS) / (1.5 * math.sqrt(DS))).astype(jnp.bfloat16)


def draw_dino_feats(key, part):
    key = jax.random.fold_in(key, 7)
    first, second, third = jax.random.split(key, 3)
    row_scale = jnp.exp(jax.random.uniform(second, (IMAGES, P_SIZE, 1), jnp.float32, -1.15, 1.15))
    base = jax.random.normal(first, (IMAGES, P_SIZE, DD), jnp.float32)
    return (base * row_scale * column_scales(third, DD) / 2.2).astype(jnp.bfloat16)


def draw_sig_feats(key, part):
    key = jax.random.fold_in(key, 8)
    first, second, third = jax.random.split(key, 3)
    row_scale = jnp.exp(jax.random.uniform(second, (IMAGES, P_SIZE, 1), jnp.float32, -1.15, 1.15))
    base = jax.random.normal(first, (IMAGES, P_SIZE, DS), jnp.float32)
    return (base * row_scale * column_scales(third, DS) / 2.2).astype(jnp.bfloat16)


def shard_levels(own_key, dims, cuts, least, top_value):
    factor_of = 1.0
    for axis_at, shards_of in cuts:
        heights = jax.random.uniform(jax.random.fold_in(jax.random.fold_in(own_key, 6), axis_at), (shards_of,), jnp.float32, least / len(cuts), top_value / len(cuts))
        factor_of = factor_of * jnp.repeat(jnp.exp(heights), dims[axis_at] // shards_of).reshape((-1,) + (1,) * (len(dims) - 1 - axis_at))
    return factor_of


def centred(own_key, shape, scale, most, cuts=(), kind=jnp.bfloat16):
    drawn = scale * jax.random.normal(own_key, shape, jnp.float32)
    if cuts:
        drawn = drawn * shard_levels(own_key, shape, cuts, -0.22, 0.18)
    return jnp.clip(drawn, -most, most).astype(kind)


def setup_inputs(seed: int = 0, part: int = 0) -> dict:
    splits = jax.random.split(jax.random.key(seed), 13)
    part_keys = jax.random.split(jax.random.fold_in(splits[12], part), 13)
    return {
        "resid": centred(part_keys[0], (IMAGES, P_SIZE, D), 1.0, 6.0, ((0, 8),)),
        "gain_mlp": jnp.clip(1.0 + 0.15 * jax.random.normal(splits[1], (D,), jnp.float32), 0.25, 1.75),
        "gain_out": jnp.clip(1.0 + 0.15 * jax.random.normal(splits[2], (D,), jnp.float32), 0.25, 1.75),
        "w_in": centred(splits[3], (D, FF), D ** -0.5, 0.15625, ((1, 2),)),
        "w_out": centred(splits[4], (FF, D), FF ** -0.5, 0.078125, ((0, 2),)),
        "a_dino": centred(splits[5], (D, DD), D ** -0.5, 0.15625, ((1, 2),)),
        "b_dino": draw_b_dino(jax.random.fold_in(splits[12], 71), part),
        "a_sig": centred(splits[7], (D, DS), D ** -0.5, 0.15625, ((1, 2),)),
        "b_sig": draw_b_sig(jax.random.fold_in(splits[12], 71), part),
        "dino_feats": draw_dino_feats(jax.random.fold_in(jax.random.fold_in(splits[12], part), 71), part),
        "sig_feats": draw_sig_feats(jax.random.fold_in(jax.random.fold_in(splits[12], part), 71), part),
        "owner": jax.random.permutation(part_keys[11], IMAGES).astype(jnp.int32),
    }


EPS = 1e-06

def layer_norm(values, gain):
    center = values - lax.optimization_barrier(jnp.mean(values, axis=-1, keepdims=True))
    spread = lax.optimization_barrier(jnp.mean(center * center, axis=-1, keepdims=True))
    return center * lax.rsqrt(spread + EPS) * gain

def norm_back(values, gain, upstream):
    center = values - lax.optimization_barrier(jnp.mean(values, axis=-1, keepdims=True))
    recip = lax.rsqrt(lax.optimization_barrier(jnp.mean(center * center, axis=-1, keepdims=True)) + EPS)
    unit = center * recip
    scaled = upstream * gain
    return recip * (scaled - lax.optimization_barrier(jnp.mean(scaled, axis=-1, keepdims=True)) - unit * lax.optimization_barrier(jnp.mean(scaled * unit, axis=-1, keepdims=True)))

def gelu_tanh(values):
    return jax.nn.gelu(values, approximate=True)

def gelu_back(values, upstream):
    _, pullback = jax.vjp(gelu_tanh, values)
    return pullback(upstream)[0]

def cosine_back(predicted, target, sq_pred, cross, sq_target, channels, factor):
    norm_pred = sq_pred + channels * EPS
    norm_target = sq_target + channels * EPS
    recip = lax.rsqrt(norm_pred * norm_target)
    cosine = cross * recip
    return factor * (predicted - target - channels * (target * recip[:, None] - (cosine / norm_pred)[:, None] * predicted))

def contract_rows(left, right):
    return lax.dot_general(left, right, (((0,), (0,)), ((), ())), preferred_element_type=jnp.float32)

def contract_cols(left, right):
    return lax.dot_general(left, right, (((1,), (1,)), ((), ())), preferred_element_type=jnp.float32)

def adaptor_terms(summary, target, a_proj, b_proj, factor):
    pre_adapt = jnp.dot(summary, a_proj, preferred_element_type=jnp.float32)
    act_adapt = gelu_tanh(pre_adapt).astype(jnp.bfloat16)
    predicted = jnp.dot(act_adapt, b_proj, preferred_element_type=jnp.float32)
    teacher = target.astype(jnp.float32)
    back_pred = cosine_back(predicted, teacher, lax.optimization_barrier(jnp.sum(predicted * predicted, axis=-1)), lax.optimization_barrier(jnp.sum(predicted * teacher, axis=-1)), lax.optimization_barrier(jnp.sum(teacher * teacher, axis=-1)), b_proj.shape[1], factor).astype(jnp.bfloat16)
    grad_b = contract_rows(act_adapt, back_pred)
    down_adapt = gelu_back(pre_adapt, contract_cols(back_pred, b_proj)).astype(jnp.bfloat16)
    grad_a = contract_rows(summary, down_adapt)
    return (grad_a, grad_b, contract_cols(down_adapt, a_proj))

def reference(resid, gain_mlp, gain_out, w_in, w_out, a_dino, b_dino, a_sig, b_sig, dino_feats, sig_feats, owner):
    slots = N_DP * N_TEACH
    factor = 1.0 / math.sqrt(IMAGES * P_SIZE)
    inverse = jnp.zeros((IMAGES,), jnp.int32).at[owner.astype(jnp.int32)].set(jnp.arange(IMAGES, dtype=jnp.int32))
    rows_all = resid.reshape(slots, IMG_DEV * P_SIZE, D)
    target_dino = dino_feats[inverse].reshape(slots, IMG_DEV * P_SIZE, DD)
    target_sig = sig_feats[inverse].reshape(slots, IMG_DEV * P_SIZE, DS)

    def block_step(totals, items):
        rows_in, tgt_dino, tgt_sig = items
        source = rows_in.astype(jnp.float32)
        normed = layer_norm(source, gain_mlp).astype(jnp.bfloat16)
        pre_act = jnp.dot(normed, w_in, preferred_element_type=jnp.float32)
        hidden = gelu_tanh(pre_act).astype(jnp.bfloat16)
        stream = source + jnp.dot(hidden, w_out, preferred_element_type=jnp.float32)
        summary = layer_norm(stream, gain_out).astype(jnp.bfloat16)
        grad_a_d, grad_b_d, up_dino = adaptor_terms(summary, tgt_dino, a_dino, b_dino, factor)
        grad_a_s, grad_b_s, up_sig = adaptor_terms(summary, tgt_sig, a_sig, b_sig, factor)
        back_stream = norm_back(stream, gain_out, up_dino + up_sig).astype(jnp.bfloat16)
        grad_wo = contract_rows(hidden, back_stream)
        back_hidden = gelu_back(pre_act, contract_cols(back_stream, w_out)).astype(jnp.bfloat16)
        grad_wi = contract_rows(normed, back_hidden)
        terms = (grad_wi, grad_wo, grad_a_d, grad_b_d, grad_a_s, grad_b_s)
        return (tuple((total + lax.optimization_barrier(term.astype(jnp.bfloat16)).astype(jnp.float32) for total, term in zip(totals, terms))), None)
    start = (jnp.zeros((D, FF), jnp.float32), jnp.zeros((FF, D), jnp.float32), jnp.zeros((D, DD), jnp.float32), jnp.zeros((DD, DD), jnp.float32), jnp.zeros((D, DS), jnp.float32), jnp.zeros((DS, DS), jnp.float32))
    totals, _ = lax.scan(block_step, start, (rows_all, target_dino, target_sig))
    return (totals[0], totals[1], totals[2], totals[3], totals[4], totals[5])
```

```python
import math

import jax
import jax.numpy as jnp
from jax import lax
from jax.sharding import PartitionSpec as P

EPS = 1e-06
ROOT = math.sqrt(2.0 / math.pi)
CUBE = 0.044715


def layer_norm(values, gain):
    center = values - jnp.mean(values, axis=-1, keepdims=True)
    spread = jnp.mean(center * center, axis=-1, keepdims=True)
    return center * lax.rsqrt(spread + EPS) * gain


def norm_back(values, gain, upstream):
    center = values - jnp.mean(values, axis=-1, keepdims=True)
    recip = lax.rsqrt(jnp.mean(center * center, axis=-1, keepdims=True) + EPS)
    unit = center * recip
    scaled = upstream * gain
    return recip * (
        scaled
        - jnp.mean(scaled, axis=-1, keepdims=True)
        - unit * jnp.mean(scaled * unit, axis=-1, keepdims=True)
    )


def gelu_and_slope(values):
    square = values * values
    bend = jnp.tanh(ROOT * values * (1.0 + CUBE * square))
    half = 0.5 * (1.0 + bend)
    slope = half + 0.5 * values * (1.0 - bend * bend) * (ROOT * (1.0 + 3.0 * CUBE * square))
    return (values * half).astype(jnp.bfloat16), slope.astype(jnp.bfloat16)


def cosine_back(predicted, target, channels, factor):
    sq_pred = jnp.sum(predicted * predicted, axis=-1, keepdims=True)
    cross = jnp.sum(predicted * target, axis=-1, keepdims=True)
    sq_target = jnp.sum(target * target, axis=-1, keepdims=True)
    norm_pred = sq_pred + channels * EPS
    norm_target = sq_target + channels * EPS
    recip = lax.rsqrt(norm_pred * norm_target)
    cosine = cross * recip
    return factor * (
        predicted - target - channels * (target * recip - (cosine / norm_pred) * predicted)
    )


def matmul(left, right):
    return jnp.dot(left, right, preferred_element_type=jnp.float32)


def contract_rows(left, right):
    return lax.dot_general(
        left, right, (((0,), (0,)), ((), ())), preferred_element_type=jnp.float32
    )


def contract_cols(left, right):
    return lax.dot_general(
        left, right, (((1,), (1,)), ((), ())), preferred_element_type=jnp.float32
    )


def shift(values, axis):
    count = lax.axis_size(axis)
    return lax.ppermute(values, axis, [(i, (i + 1) % count) for i in range(count)])


def ring_gather(values, axis):
    held = [values]
    for _ in range(lax.axis_size(axis) - 1):
        held.append(shift(held[-1], axis))
    return held


def ring_sum(blocks, axis):
    count = lax.axis_size(axis)
    me = lax.axis_index(axis)

    def block(i):
        return lax.dynamic_index_in_dim(blocks, lax.rem(i + 2 * count, count), 0, keepdims=False)

    held = block(me - 1)
    for step in range(1, count):
        got = shift(held, axis).astype(jnp.float32)
        total = got + block(me - 1 - step).astype(jnp.float32)
        held = total.astype(jnp.bfloat16)
    return total if count > 1 else held.astype(jnp.float32)


def core_sum(blocks):
    count = lax.axis_size("teach")
    if count != 2:
        return lax.psum_scatter(blocks, "teach", scatter_dimension=1, tiled=False)
    me = lax.axis_index("teach")
    mine = lax.dynamic_index_in_dim(blocks, me, 1, keepdims=False)
    theirs = lax.dynamic_index_in_dim(blocks, 1 - me, 1, keepdims=False)
    got = shift(theirs, "teach")
    return (mine.astype(jnp.float32) + got.astype(jnp.float32)).astype(jnp.bfloat16)


def sum_mp(part):
    if lax.axis_size("mp") == 2:
        return part.astype(jnp.float32) + shift(part, "mp").astype(jnp.float32)
    return lax.psum(part, "mp").astype(jnp.float32)


def join_mp(values, axis):
    if lax.axis_size("mp") != 2:
        return lax.all_gather(values, "mp", axis=axis, tiled=True)
    other = shift(values, "mp")
    return in_order(values, other, axis)


def in_order(own, other, axis):
    first = lax.axis_index("mp") == 0
    return jnp.concatenate(
        [jnp.where(first, own, other), jnp.where(first, other, own)], axis=axis
    )


def own_teacher(feats, inverse):
    sent = feats.at[inverse].get(mode="promise_in_bounds", unique_indices=True)
    got = lax.all_to_all(sent, ("dp", "teach"), split_axis=0, concat_axis=1, tiled=True)
    return join_mp(got.reshape(-1, feats.shape[2]), 1)


def gather_back(part, stream, gain):
    if lax.axis_size("mp") != 2:
        own = norm_back(stream, gain, sum_mp(part)).astype(jnp.bfloat16)
        return ring_gather(own, "dp")
    me = lax.axis_index("mp")
    half = part.shape[0] // 2
    mine = lax.dynamic_slice_in_dim(part, me * half, half, 0)
    theirs = lax.dynamic_slice_in_dim(part, (1 - me) * half, half, 0)
    upstream = mine.astype(jnp.float32) + shift(theirs, "mp").astype(jnp.float32)
    rows = lax.dynamic_slice_in_dim(stream, me * half, half, 0)
    back = norm_back(rows, gain, upstream).astype(jnp.bfloat16)
    return [in_order(held, shift(held, "mp"), 0) for held in ring_gather(back, "dp")]


def per_device(
    resid,
    gain_mlp,
    gain_out,
    w_in,
    w_out,
    a_dino,
    b_dino,
    a_sig,
    b_sig,
    dino_feats,
    sig_feats,
    owner,
):
    n_chips = lax.axis_size("dp")
    n_cores = lax.axis_size("teach")
    width = resid.shape[2]
    rows = resid.shape[0] * resid.shape[1]
    factor = 1.0 / math.sqrt(n_chips * n_cores * rows)
    total_images = owner.shape[0]
    chip = lax.axis_index("dp")
    core = lax.axis_index("teach")

    source = resid.reshape(rows, width).astype(jnp.float32)
    normed = layer_norm(source, gain_mlp).astype(jnp.bfloat16)
    all_normed = ring_gather(normed, "dp")

    inverse = (
        jnp.zeros((total_images,), jnp.int32)
        .at[owner]
        .set(jnp.arange(total_images, dtype=jnp.int32))
    )
    teacher_dino = own_teacher(dino_feats, inverse)
    teacher_sig = own_teacher(sig_feats, inverse)

    hidden, slope = gelu_and_slope(matmul(normed, w_in))
    stream = source + sum_mp(matmul(hidden, w_out).astype(jnp.bfloat16))
    summary = layer_norm(stream, gain_out).astype(jnp.bfloat16)

    act_dino, slope_dino = gelu_and_slope(matmul(summary, a_dino))
    act_sig, slope_sig = gelu_and_slope(matmul(summary, a_sig))
    pred_dino = sum_mp(matmul(act_dino, b_dino).astype(jnp.bfloat16))
    pred_sig = sum_mp(matmul(act_sig, b_sig).astype(jnp.bfloat16))

    back_dino = cosine_back(
        pred_dino, teacher_dino.astype(jnp.float32), b_dino.shape[1], factor
    ).astype(jnp.bfloat16)
    back_sig = cosine_back(
        pred_sig, teacher_sig.astype(jnp.float32), b_sig.shape[1], factor
    ).astype(jnp.bfloat16)
    down_dino = (slope_dino * contract_cols(back_dino, b_dino)).astype(jnp.bfloat16)
    down_sig = (slope_sig * contract_cols(back_sig, b_sig)).astype(jnp.bfloat16)
    part = (contract_cols(down_dino, a_dino) + contract_cols(down_sig, a_sig)).astype(
        jnp.bfloat16
    )
    backs = jnp.concatenate(gather_back(part, stream, gain_out), axis=0)

    def blocks(grad):
        return grad.astype(jnp.bfloat16).reshape(n_chips, n_cores, -1, grad.shape[1])

    grad_b_d = blocks(contract_rows(back_dino, act_dino))
    grad_b_s = blocks(contract_rows(back_sig, act_sig))
    wide, narrow = grad_b_d.shape[3], grad_b_s.shape[3]
    cut = grad_b_d.shape[2]
    grad_b = jnp.concatenate(
        [grad_b_d, jnp.pad(grad_b_s, ((0, 0), (0, 0), (0, 0), (0, wide - narrow)))], axis=2
    )
    grad_b = ring_sum(core_sum(grad_b), "dp")
    out_b_d = grad_b[:cut].T
    out_b_s = grad_b[cut:, :narrow].T
    grad_a = jnp.concatenate(
        [contract_rows(summary, down_dino), contract_rows(summary, down_sig)], axis=1
    )
    grad_a = ring_sum(core_sum(blocks(grad_a)), "dp")
    out_a_d = grad_a[:, : down_dino.shape[1]]
    out_a_s = grad_a[:, down_dino.shape[1] :]

    others = jnp.concatenate(all_normed[1:], axis=0)
    other_hidden, other_slope = gelu_and_slope(matmul(others, w_in))
    normeds = jnp.concatenate([normed, others], axis=0)
    hiddens = jnp.concatenate([hidden, other_hidden], axis=0)
    slopes = jnp.concatenate([slope, other_slope], axis=0)
    back_hidden = (slopes * contract_cols(backs, w_out)).astype(jnp.bfloat16)
    share = width // (n_chips * n_cores)

    def shares(values):
        at = chip * n_cores + core
        own = lax.dynamic_slice_in_dim(values, at * share, share, 1)
        peer = chip * n_cores + (1 - core)
        return own, lax.dynamic_slice_in_dim(values, peer * share, share, 1)

    own_n, peer_n = shares(normeds)
    own_s, peer_s = shares(backs)
    sent_out = contract_rows(hiddens, peer_s).astype(jnp.bfloat16)
    got_out = shift(sent_out, "teach")
    sent_in = contract_rows(peer_n, back_hidden).astype(jnp.bfloat16)
    got_in = shift(sent_in, "teach")
    out_wo = contract_rows(hiddens, own_s) + got_out.astype(jnp.float32)
    out_wi = contract_rows(own_n, back_hidden) + got_in.astype(jnp.float32)
    return out_wi, out_wo, out_a_d, out_b_d, out_a_s, out_b_s


def solution(mesh):
    placed = (
        P(("groups", "dp", "teach"), None, None),
        P(),
        P(),
        P(None, "mp"),
        P("mp", None),
        P(None, "mp"),
        P("mp", None),
        P(None, "mp"),
        P("mp", None),
        P("groups", ("dp", "teach"), "mp"),
        P("groups", ("dp", "teach"), "mp"),
        P("groups"),
    )
    return jax.shard_map(
        per_device,
        mesh=mesh,
        in_specs=placed,
        out_specs=(
            P(("groups", "dp", "teach"), "mp"),
            P(("groups", "mp"), ("dp", "teach")),
            P(("groups", "dp", "teach"), "mp"),
            P(("groups", "mp"), ("dp", "teach")),
            P(("groups", "dp", "teach"), "mp"),
            P(("groups", "mp"), ("dp", "teach")),
        ),
        check_vma=False,
    )
```

```python
import math

import jax
import jax.numpy as jnp
from jax import lax
from jax.sharding import PartitionSpec as P

EPS = 1e-06
ROOT = math.sqrt(2.0 / math.pi)
CUBE = 0.044715


def layer_norm(values, gain):
    center = values - jnp.mean(values, axis=-1, keepdims=True)
    spread = jnp.mean(center * center, axis=-1, keepdims=True)
    return center * lax.rsqrt(spread + EPS) * gain


def norm_back(values, gain, upstream):
    center = values - jnp.mean(values, axis=-1, keepdims=True)
    recip = lax.rsqrt(jnp.mean(center * center, axis=-1, keepdims=True) + EPS)
    unit = center * recip
    scaled = upstream * gain
    return recip * (
        scaled
        - jnp.mean(scaled, axis=-1, keepdims=True)
        - unit * jnp.mean(scaled * unit, axis=-1, keepdims=True)
    )


def gelu_and_slope(values):
    square = values * values
    bend = jnp.tanh(ROOT * values * (1.0 + CUBE * square))
    half = 0.5 * (1.0 + bend)
    slope = half + 0.5 * values * (1.0 - bend * bend) * (ROOT * (1.0 + 3.0 * CUBE * square))
    return (values * half).astype(jnp.bfloat16), slope.astype(jnp.bfloat16)


def cosine_back(predicted, target, channels, factor):
    sq_pred = jnp.sum(predicted * predicted, axis=-1, keepdims=True)
    cross = jnp.sum(predicted * target, axis=-1, keepdims=True)
    sq_target = jnp.sum(target * target, axis=-1, keepdims=True)
    norm_pred = sq_pred + channels * EPS
    norm_target = sq_target + channels * EPS
    recip = lax.rsqrt(norm_pred * norm_target)
    cosine = cross * recip
    return factor * (
        predicted - target - channels * (target * recip - (cosine / norm_pred) * predicted)
    )


def matmul(left, right):
    return jnp.dot(left, right, preferred_element_type=jnp.float32)


def contract_rows(left, right):
    return lax.dot_general(
        left, right, (((0,), (0,)), ((), ())), preferred_element_type=jnp.float32
    )


def contract_cols(left, right):
    return lax.dot_general(
        left, right, (((1,), (1,)), ((), ())), preferred_element_type=jnp.float32
    )


def shift(values, axis, by=1):
    count = lax.axis_size(axis)
    return lax.ppermute(values, axis, [(i, (i + by) % count) for i in range(count)])


def core_sum(blocks):
    count = lax.axis_size("teach")
    if count != 2:
        return lax.psum_scatter(blocks, "teach", scatter_dimension=1, tiled=False)
    me = lax.axis_index("teach")
    mine = lax.dynamic_index_in_dim(blocks, me, 1, keepdims=False)
    theirs = lax.dynamic_index_in_dim(blocks, 1 - me, 1, keepdims=False)
    got = shift(theirs, "teach")
    return (mine.astype(jnp.float32) + got.astype(jnp.float32)).astype(jnp.bfloat16)


def sum_mp(part):
    if lax.axis_size("mp") == 2:
        return part.astype(jnp.float32) + shift(part, "mp").astype(jnp.float32)
    return lax.psum(part, "mp").astype(jnp.float32)


def join_mp(values, axis):
    if lax.axis_size("mp") != 2:
        return lax.all_gather(values, "mp", axis=axis, tiled=True)
    other = shift(values, "mp")
    return in_order(values, other, axis)


def in_order(own, other, axis):
    first = lax.axis_index("mp") == 0
    return jnp.concatenate(
        [jnp.where(first, own, other), jnp.where(first, other, own)], axis=axis
    )


def tie(*values):
    return lax.optimization_barrier(values)


def swap_pair(values, axis):
    count = lax.axis_size(axis)
    return lax.ppermute(values, axis, [(i, i ^ 1) for i in range(count)])


def paired(values, axis):
    got = swap_pair(values, axis)
    even = lax.rem(lax.axis_index(axis), 2) == 0
    return jnp.concatenate([jnp.where(even, values, got), jnp.where(even, got, values)], axis=0)


def first_part(weights, axes):
    at = 0
    for axis in reversed(axes):
        at = at * 2 + lax.rem(lax.axis_index(axis), 2)
    rows = weights.shape[0] // 2 ** len(axes)
    return lax.dynamic_slice_in_dim(weights, at * rows, rows, 0)


def gather_parts(held, axes):
    for axis in axes:
        held = paired(held, axis)
    return held


def back_rows(part, stream, gain):
    if lax.axis_size("mp") != 2:
        return norm_back(stream, gain, sum_mp(part)).astype(jnp.bfloat16)
    me = lax.axis_index("mp")
    half = part.shape[0] // 2
    mine = lax.dynamic_slice_in_dim(part, me * half, half, 0)
    theirs = lax.dynamic_slice_in_dim(part, (1 - me) * half, half, 0)
    upstream = mine.astype(jnp.float32) + shift(theirs, "mp").astype(jnp.float32)
    rows = lax.dynamic_slice_in_dim(stream, me * half, half, 0)
    return norm_back(rows, gain, upstream).astype(jnp.bfloat16)


def whole_rows(held):
    return in_order(held, shift(held, "mp"), 0) if lax.axis_size("mp") == 2 else held


def per_device(
    resid,
    gain_mlp,
    gain_out,
    w_in,
    w_out,
    a_dino,
    b_dino,
    a_sig,
    b_sig,
    dino_feats,
    sig_feats,
    owner,
):
    n_chips = lax.axis_size("dp")
    n_cores = lax.axis_size("teach")
    width = resid.shape[2]
    rows = resid.shape[0] * resid.shape[1]
    factor = 1.0 / math.sqrt(n_chips * n_cores * rows)
    total_images = owner.shape[0]
    chip = lax.axis_index("dp")
    core = lax.axis_index("teach")

    two = lax.axis_size("mp") == 2
    inverse = (
        jnp.zeros((total_images,), jnp.int32)
        .at[owner]
        .set(jnp.arange(total_images, dtype=jnp.int32))
    )
    sent = jnp.concatenate([dino_feats, sig_feats], axis=2)
    sent = sent.at[inverse].get(mode="promise_in_bounds", unique_indices=True)
    resid, sent = tie(resid, sent)
    got = lax.all_to_all(sent, ("dp", "teach"), split_axis=0, concat_axis=1, tiled=True)
    got = got.reshape(rows, -1)
    if two:
        first_b_dino = first_part(b_dino, ("dp", "groups", "teach"))
        first_b_sig = first_part(b_sig, ("groups", "teach"))
        resid, first_b_dino, first_b_sig = tie(resid, first_b_dino, first_b_sig)
        first_b_dino = shift(first_b_dino, "mp")
        first_b_sig = shift(first_b_sig, "mp")
    source = resid.reshape(rows, width).astype(jnp.float32)
    normed = layer_norm(source, gain_mlp).astype(jnp.bfloat16)
    normed_sent, got = tie(normed, got)
    others = [shift(normed_sent, "dp", -k) for k in range(1, n_chips)]
    hidden, slope = gelu_and_slope(matmul(normed, w_in))
    out_part = matmul(hidden, w_out).astype(jnp.bfloat16)

    dino_part = dino_feats.shape[2]

    stream = source + sum_mp(out_part)
    summary = layer_norm(stream, gain_out).astype(jnp.bfloat16)
    act_dino, slope_dino = gelu_and_slope(matmul(summary, a_dino))
    act_sig, slope_sig = gelu_and_slope(matmul(summary, a_sig))
    if two:
        peer_act_dino = shift(act_dino, "mp")
        peer_act_sig = shift(act_sig, "mp")
        peer_b_dino = gather_parts(first_b_dino, ("dp", "groups", "teach"))
        peer_b_sig = gather_parts(first_b_sig, ("groups", "teach"))
        got_sent, summary = tie(got, summary)
        peer_got = shift(got_sent, "mp")
        teacher_dino = in_order(got[:, :dino_part], peer_got[:, :dino_part], 1)
        teacher_sig = in_order(got[:, dino_part:], peer_got[:, dino_part:], 1)
    else:
        teacher_dino = join_mp(got[:, :dino_part], 1)
        teacher_sig = join_mp(got[:, dino_part:], 1)
    if two:
        pred_dino = matmul(act_dino, b_dino) + matmul(peer_act_dino, peer_b_dino)
        pred_sig = matmul(act_sig, b_sig) + matmul(peer_act_sig, peer_b_sig)
    else:
        pred_dino = sum_mp(matmul(act_dino, b_dino).astype(jnp.bfloat16))
        pred_sig = sum_mp(matmul(act_sig, b_sig).astype(jnp.bfloat16))

    back_dino = cosine_back(pred_dino, teacher_dino.astype(jnp.float32), b_dino.shape[1], factor).astype(jnp.bfloat16)
    back_sig = cosine_back(pred_sig, teacher_sig.astype(jnp.float32), b_sig.shape[1], factor).astype(jnp.bfloat16)
    down_dino = (slope_dino * contract_cols(back_dino, b_dino)).astype(jnp.bfloat16)
    down_sig = (slope_sig * contract_cols(back_sig, b_sig)).astype(jnp.bfloat16)
    part = (contract_cols(down_dino, a_dino) + contract_cols(down_sig, a_sig)).astype(
        jnp.bfloat16
    )
    back = back_rows(part, stream, gain_out)

    def blocks(grad):
        return grad.astype(jnp.bfloat16).reshape(n_chips, n_cores, -1, grad.shape[1])

    grad_b_d = blocks(contract_rows(back_dino, act_dino))
    grad_b_s = blocks(contract_rows(back_sig, act_sig))
    wide, narrow = grad_b_d.shape[3], grad_b_s.shape[3]
    cut = grad_b_d.shape[2]
    grad_b = jnp.concatenate(
        [grad_b_d, jnp.pad(grad_b_s, ((0, 0), (0, 0), (0, 0), (0, wide - narrow)))], axis=2
    )
    chip_b = core_sum(grad_b)
    back, chip_b = tie(back, chip_b)
    grad_a = jnp.concatenate(
        [contract_rows(summary, down_dino), contract_rows(summary, down_sig)], axis=1
    )
    chip_a = core_sum(blocks(grad_a))

    def block(values, i):
        return lax.dynamic_index_in_dim(values, lax.rem(i + 2 * n_chips, n_chips), 0, keepdims=False)

    def ring_step(held, total, chip_sums, step):
        got = shift(held, "dp")
        total = got.astype(jnp.float32) + block(chip_sums, chip - 1 - step).astype(jnp.float32)
        return total.astype(jnp.bfloat16), total

    held_s = [back]
    held_b, held_a = block(chip_b, chip - 1), block(chip_a, chip - 1)
    total_b, total_a = held_b.astype(jnp.float32), held_a.astype(jnp.float32)
    held_s += [shift(back, "dp", -k) for k in range(1, n_chips)]
    for step in range(1, n_chips):
        held_b, total_b = ring_step(held_b, total_b, chip_b, step)
        if step == 1:
            held_s[1], held_b, held_a = tie(held_s[1], held_b, held_a)
        held_a, total_a = ring_step(held_a, total_a, chip_a, step)
    backs = jnp.concatenate([whole_rows(held) for held in held_s], axis=0)
    out_b_d = total_b[:cut].T
    out_b_s = total_b[cut:, :narrow].T
    out_a_d = total_a[:, : down_dino.shape[1]]
    out_a_s = total_a[:, down_dino.shape[1] :]

    others = jnp.concatenate(others, axis=0)
    others, _ = tie(others, held_s[1])
    normeds = jnp.concatenate([normed, others], axis=0)
    other_hidden, other_slope = gelu_and_slope(matmul(others, w_in))
    hiddens = jnp.concatenate([hidden, other_hidden], axis=0)
    slopes = jnp.concatenate([slope, other_slope], axis=0)
    back_hidden = (slopes * contract_cols(backs, w_out)).astype(jnp.bfloat16)
    share = width // (n_chips * n_cores)

    def shares(values):
        at = chip * n_cores + core
        own = lax.dynamic_slice_in_dim(values, at * share, share, 1)
        peer = chip * n_cores + (1 - core)
        return own, lax.dynamic_slice_in_dim(values, peer * share, share, 1)

    own_n, peer_n = shares(normeds)
    own_s, peer_s = shares(backs)
    sent_out = contract_rows(hiddens, peer_s).astype(jnp.bfloat16)
    got_out = shift(sent_out, "teach")
    sent_in = contract_rows(peer_n, back_hidden).astype(jnp.bfloat16)
    got_in = shift(sent_in, "teach")
    out_wo = contract_rows(hiddens, own_s) + got_out.astype(jnp.float32)
    out_wi = contract_rows(own_n, back_hidden) + got_in.astype(jnp.float32)
    return out_wi, out_wo, out_a_d, out_b_d, out_a_s, out_b_s


def solution(mesh):
    placed = (
        P(("groups", "dp", "teach"), None, None),
        P(),
        P(),
        P(None, "mp"),
        P("mp", None),
        P(None, "mp"),
        P("mp", None),
        P(None, "mp"),
        P("mp", None),
        P("groups", ("dp", "teach"), "mp"),
        P("groups", ("dp", "teach"), "mp"),
        P("groups"),
    )
    return jax.shard_map(
        per_device,
        mesh=mesh,
        in_specs=placed,
        out_specs=(
            P(("groups", "dp", "teach"), "mp"),
            P(("groups", "mp"), ("dp", "teach")),
            P(("groups", "dp", "teach"), "mp"),
            P(("groups", "mp"), ("dp", "teach")),
            P(("groups", "dp", "teach"), "mp"),
            P(("groups", "mp"), ("dp", "teach")),
        ),
        check_vma=False,
    )
```

```python
import math

import jax
import jax.numpy as jnp
from jax import lax
from jax.experimental import pallas as pl
from jax.experimental.pallas import tpu as pltpu
from jax.sharding import PartitionSpec as P

EPS = 1e-06
ROOT = math.sqrt(2.0 / math.pi)
CUBE = 0.044715


def layer_norm(values, gain):
    center = values - jnp.mean(values, axis=-1, keepdims=True)
    spread = jnp.mean(center * center, axis=-1, keepdims=True)
    return center * lax.rsqrt(spread + EPS) * gain


def norm_back(values, gain, upstream):
    center = values - jnp.mean(values, axis=-1, keepdims=True)
    recip = lax.rsqrt(jnp.mean(center * center, axis=-1, keepdims=True) + EPS)
    unit = center * recip
    scaled = upstream * gain
    return recip * (
        scaled
        - jnp.mean(scaled, axis=-1, keepdims=True)
        - unit * jnp.mean(scaled * unit, axis=-1, keepdims=True)
    )


def gelu_and_slope(values):
    square = values * values
    bend = jnp.tanh(ROOT * values * (1.0 + CUBE * square))
    half = 0.5 * (1.0 + bend)
    slope = half + 0.5 * values * (1.0 - bend * bend) * (ROOT * (1.0 + 3.0 * CUBE * square))
    return (values * half).astype(jnp.bfloat16), slope.astype(jnp.bfloat16)


def tiles(count, step=256):
    return [(at, min(at + step, count)) for at in range(0, count, step)]


def in_vmem(count):
    return [pl.BlockSpec(memory_space=pltpu.VMEM)] * count


def row_dot(left, right):
    return lax.dot_general(
        left, right, (((1,), (1,)), ((), ())), preferred_element_type=jnp.float32
    )


def params(flops, nbytes, room=8):
    return dict(
        compiler_params=pltpu.CompilerParams(vmem_limit_bytes=room * 1024 * 1024),
        cost_estimate=pl.CostEstimate(flops=flops, bytes_accessed=nbytes, transcendentals=0),
    )


def mlp_forward(resid, gain, w_in, w_out):
    rows, width = resid.shape
    units = w_in.shape[1]
    tile = next(t for t in (512, 256, 128, units) if units % t == 0)
    steps = units // tile

    def kernel(resid_ref, gain_ref, w_in_hbm, w_out_hbm, normed_ref, hid_ref, slope_ref, out_ref, w_in_ref, w_out_ref, total, in_sem, out_sem):
        def copies(at):
            cut = pl.ds(at * tile, tile)
            return (
                pltpu.make_async_copy(w_in_hbm.at[:, cut], w_in_ref.at[:, cut], in_sem.at[at]),
                pltpu.make_async_copy(w_out_hbm.at[cut, :], w_out_ref.at[cut, :], out_sem.at[at]),
            )

        for at in range(steps):
            for copy in copies(at):
                copy.start()
        normed_ref[...] = layer_norm(resid_ref[...].astype(jnp.float32), gain_ref[...]).astype(jnp.bfloat16)
        for at in range(steps):
            lo, hi = at * tile, (at + 1) * tile
            into, out_of = copies(at)
            into.wait()
            for left, right in tiles(tile):
                hidden, slope = gelu_and_slope(matmul(normed_ref[...], w_in_ref[:, lo + left : lo + right]))
                hid_ref[:, lo + left : lo + right] = hidden
                slope_ref[:, lo + left : lo + right] = slope
            out_of.wait()
            for left, right in tiles(width):
                value = matmul(hid_ref[:, lo:hi], w_out_ref[lo:hi, left:right])
                if at:
                    value = value + total[:, left:right]
                if at < steps - 1:
                    total[:, left:right] = value
                else:
                    out_ref[:, left:right] = value.astype(jnp.bfloat16)

    shape = lambda *dims: jax.ShapeDtypeStruct(dims, jnp.bfloat16)
    return pl.pallas_call(
        kernel,
        in_specs=in_vmem(2) + [pl.BlockSpec(memory_space=pltpu.HBM)] * 2,
        out_specs=in_vmem(4),
        out_shape=[shape(rows, width), shape(rows, units), shape(rows, units), shape(rows, width)],
        scratch_shapes=[
            pltpu.VMEM((width, units), jnp.bfloat16),
            pltpu.VMEM((units, width), jnp.bfloat16),
            pltpu.VMEM((rows, width), jnp.float32),
            pltpu.SemaphoreType.DMA((steps,)),
            pltpu.SemaphoreType.DMA((steps,)),
        ],
        **params(4 * rows * width * units, 4 * width * units, 54),
    )(resid, gain.reshape(1, -1), w_in, w_out)


def route_features(info, owner, own, peer):
    images, patches, _ = own[0].shape
    n_chips = images // 2
    channels = 2 * sum(part.shape[2] for part in own)

    def kernel(info_ref, owner_ref, own_d, own_s, peer_d, peer_s, mine_ref, theirs_ref):
        core, chip, first = info_ref[0], info_ref[1], info_ref[2] == 0

        def one(image, carry):
            to = owner_ref[image]
            place = lax.rem(to // 2 - chip + n_chips, n_chips)
            pieces = []
            for here, there in ((own_d, peer_d), (own_s, peer_s)):
                a, b = here[image], there[image]
                pieces += [jnp.where(first, a, b), jnp.where(first, b, a)]
            joined = jnp.concatenate(pieces, axis=-1)

            @pl.when(lax.rem(to, 2) == core)
            def _():
                mine_ref[place] = joined

            @pl.when(lax.rem(to, 2) != core)
            def _():
                theirs_ref[place] = joined

            return carry

        lax.fori_loop(0, images, one, 0)

    return pl.pallas_call(
        kernel,
        in_specs=[pl.BlockSpec(memory_space=pltpu.SMEM)] * 2 + in_vmem(4),
        out_specs=in_vmem(2),
        out_shape=[jax.ShapeDtypeStruct((n_chips, patches, channels), jnp.bfloat16)] * 2,
        **params(images * patches * channels, 4 * images * patches * channels),
    )(info, owner, *own, *peer)


def pair_up(mine, theirs):
    n_chips, patches, channels = mine.shape

    def kernel(mine_ref, theirs_ref, *refs):
        for at, ref in enumerate(refs):
            ref[0] = mine_ref[at]
            ref[1] = theirs_ref[at]

    return pl.pallas_call(
        kernel,
        in_specs=in_vmem(2),
        out_specs=in_vmem(n_chips),
        out_shape=[jax.ShapeDtypeStruct((2, patches, channels), jnp.bfloat16)] * n_chips,
        **params(n_chips * patches * channels, 8 * n_chips * patches * channels),
    )(mine, theirs)


def adaptors_forward(resid, addends, gain, a_dino, a_sig, b_dino, b_sig):
    rows, width = resid.shape
    count = len(addends)
    wide, narrow = a_dino.shape[1], a_sig.shape[0]

    def kernel(resid_ref, gain_ref, ad_ref, as_ref, bd_ref, bs_ref, *refs):
        stream = resid_ref[...].astype(jnp.float32)
        added = refs[0][...].astype(jnp.float32)
        for ref in refs[1:count]:
            added = added + ref[...].astype(jnp.float32)
        stream = stream + added
        stream_ref, summary_ref, act_ref, slope_ref, pred_d, pred_s = refs[count:]
        stream_ref[...] = stream
        summary_ref[...] = layer_norm(stream, gain_ref[...]).astype(jnp.bfloat16)
        for lo, hi in tiles(narrow):
            act, slope = gelu_and_slope(row_dot(summary_ref[...], as_ref[lo:hi, :]))
            act_ref[:, wide + lo : wide + hi] = act
            slope_ref[:, wide + lo : wide + hi] = slope
        for lo, hi in tiles(bs_ref.shape[1]):
            pred_s[:, lo:hi] = matmul(act_ref[:, wide:], bs_ref[:, lo:hi]).astype(jnp.bfloat16)
        for lo, hi in tiles(wide):
            act, slope = gelu_and_slope(matmul(summary_ref[...], ad_ref[:, lo:hi]))
            act_ref[:, lo:hi] = act
            slope_ref[:, lo:hi] = slope
        for lo, hi in tiles(bd_ref.shape[1]):
            pred_d[:, lo:hi] = matmul(act_ref[:, :wide], bd_ref[:, lo:hi]).astype(jnp.bfloat16)

    shape = lambda cols, dtype=jnp.bfloat16: jax.ShapeDtypeStruct((rows, cols), dtype)
    work = width * (wide + narrow) + b_dino.size + b_sig.size
    return pl.pallas_call(
        kernel,
        in_specs=in_vmem(6 + count),
        out_specs=in_vmem(6),
        out_shape=[
            shape(width, jnp.float32),
            shape(width),
            shape(wide + narrow),
            shape(wide + narrow),
            shape(b_dino.shape[1]),
            shape(b_sig.shape[1]),
        ],
        **params(2 * rows * work, 2 * work),
    )(resid, gain.reshape(1, -1), a_dino, a_sig, b_dino, b_sig, *addends)


def loss_rows(info_ref, addends, targets, start, back_ref, factor):
    rows, channels = back_ref.shape
    core, chip = info_ref[0], info_ref[1]
    n_from, patches = len(targets), targets[0].shape[-2]

    def block(here, goal):
        goal = goal.astype(jnp.float32)
        value = addends[0][here, :].astype(jnp.float32)
        for ref in addends[1:]:
            value = value + ref[here, :].astype(jnp.float32)
        norm_pred = jnp.sum(value * value, axis=-1, keepdims=True) + channels * EPS
        norm_target = jnp.sum(goal * goal, axis=-1, keepdims=True) + channels * EPS
        recip = lax.rsqrt(norm_pred * norm_target)
        cosine = jnp.sum(value * goal, axis=-1, keepdims=True) * recip
        of_pred = factor * (1.0 + channels * (cosine / norm_pred))
        of_target = factor * (1.0 + channels * recip)
        back_ref[here, :] = (value * of_pred - goal * of_target).astype(jnp.bfloat16)

    for at, ref in enumerate(targets):
        if len(ref.shape) == 2:
            for lo, hi in tiles(rows, 32):
                block(slice(lo, hi), ref[lo:hi, start : start + channels])
            continue
        source = lax.rem(chip - at + n_from, n_from)
        for other in range(2):
            place = 2 * source + (1 - core if other else core)
            here = pl.ds(pl.multiple_of(place * patches, patches), patches)
            block(here, ref[other, :, start : start + channels])


def loss_gradient(info, addends, targets, start, factor):
    rows, channels = addends[0].shape
    count = len(addends)

    def kernel(info_ref, *refs):
        loss_rows(info_ref, refs[:count], refs[count:-1], start, refs[-1], factor)

    return pl.pallas_call(
        kernel,
        in_specs=[pl.BlockSpec(memory_space=pltpu.SMEM)] + in_vmem(count + len(targets)),
        out_specs=pl.BlockSpec(memory_space=pltpu.VMEM),
        out_shape=jax.ShapeDtypeStruct((rows, channels), jnp.bfloat16),
        **params(20 * rows * channels, 8 * rows * channels),
    )(info, *addends, *targets)


def adaptors_back(info, addends, targets, back_s, b_weights, slope, a_weights, factor):
    rows, channels = addends[0].shape
    width = a_weights[0].shape[0]
    units = [w.shape[0] for w in b_weights]
    count = len(addends) + len(targets)

    def kernel(info_ref, *refs):
        back_s, b_d, b_s, slope_ref, a_d, a_s, back_d, down_ref, part_ref = refs[count:]
        loss_rows(info_ref, refs[: len(addends)], refs[len(addends) : count], 0, back_d, factor)
        start = 0
        for back, weights in ((back_d, b_d), (back_s, b_s)):
            for lo, hi in tiles(weights.shape[0]):
                grown = row_dot(back[...], weights[lo:hi, :])
                down = slope_ref[:, start + lo : start + hi].astype(jnp.float32) * grown
                down_ref[:, start + lo : start + hi] = down.astype(jnp.bfloat16)
            start += weights.shape[0]
        for lo, hi in tiles(width):
            total = row_dot(down_ref[:, : units[0]], a_d[lo:hi, :])
            total = total + matmul(down_ref[:, units[0] :], a_s[:, lo:hi])
            part_ref[:, lo:hi] = total.astype(jnp.bfloat16)

    work = sum(u * (w.shape[1] + width) for u, w in zip(units, b_weights))
    shape = lambda cols: jax.ShapeDtypeStruct((rows, cols), jnp.bfloat16)
    return pl.pallas_call(
        kernel,
        in_specs=[pl.BlockSpec(memory_space=pltpu.SMEM)] + in_vmem(count + 6),
        out_specs=in_vmem(3),
        out_shape=[shape(channels), shape(sum(units)), shape(width)],
        **params(2 * rows * work, 2 * work),
    )(info, *addends, *targets, back_s, *b_weights, slope, *a_weights)


def gradient_blocks(core, pairs, n_blocks):
    rows = pairs[0][0].shape[0]
    depths = [left.shape[1] // n_blocks for left, _, _ in pairs]
    depth = max(depths)
    widths = [cols.stop - cols.start for _, _, cols in pairs]
    count = len(pairs)

    def kernel(core_ref, *refs):
        own = core_ref[0]
        mine_ref, theirs_ref = refs[2 * count :]

        def put(value, at, per, start):
            row = at
            while row < at + value.shape[0]:
                block, inside = row // per, row % per
                stop = min(at + value.shape[0], (block + 1) * per)
                piece = value[row - at : stop - at]
                place = (block // 2, slice(inside, inside + stop - row), slice(start, start + value.shape[1]))

                @pl.when(own == block % 2)
                def _():
                    mine_ref[place] = piece

                @pl.when(own != block % 2)
                def _():
                    theirs_ref[place] = piece

                row = stop

        start = 0
        for at, (per, width) in enumerate(zip(depths, widths)):
            left, right, cols = refs[2 * at], refs[2 * at + 1], pairs[at][2]
            if per < depth:
                blank = jnp.zeros((n_blocks // 2, depth - per, width), jnp.bfloat16)
                mine_ref[:, per:, start : start + width] = blank
                theirs_ref[:, per:, start : start + width] = blank
            for lo, hi in tiles(left.shape[1]):
                value = lax.dot_general(
                    left[:, lo:hi], right[:, cols], (((0,), (0,)), ((), ())), preferred_element_type=jnp.float32
                )
                put(value.astype(jnp.bfloat16), lo, per, start)
            start += width

    work = rows * sum(left.shape[1] * width for (left, _, _), width in zip(pairs, widths))
    return pl.pallas_call(
        kernel,
        in_specs=[pl.BlockSpec(memory_space=pltpu.SMEM)] + in_vmem(2 * count),
        out_specs=in_vmem(2),
        out_shape=[jax.ShapeDtypeStruct((n_blocks // 2, depth, sum(widths)), jnp.bfloat16)] * 2,
        **params(2 * work, 2 * n_blocks * depth * sum(widths)),
    )(core.astype(jnp.int32).reshape(1), *[array for pair in pairs for array in pair[:2]])


def matmul(left, right):
    return jnp.dot(left, right, preferred_element_type=jnp.float32)


def contract_rows(left, right):
    return lax.dot_general(
        left, right, (((0,), (0,)), ((), ())), preferred_element_type=jnp.float32
    )


def contract_cols(left, right):
    return lax.dot_general(
        left, right, (((1,), (1,)), ((), ())), preferred_element_type=jnp.float32
    )


def shift(values, axis, by=1):
    count = lax.axis_size(axis)
    return lax.ppermute(values, axis, [(i, (i + by) % count) for i in range(count)])


def addends_mp(part):
    if lax.axis_size("mp") == 2:
        return (part, shift(part, "mp"))
    return (lax.psum(part, "mp"),)


def in_order(own, other, axis):
    first = lax.axis_index("mp") == 0
    return jnp.concatenate(
        [jnp.where(first, own, other), jnp.where(first, other, own)], axis=axis
    )


def tie(*values):
    return lax.optimization_barrier(values)


def back_rows(place, stream, part, other, gain):
    half, width = other.shape

    def kernel(place_ref, stream_ref, part_ref, other_ref, gain_ref, back_ref):
        here = pl.ds(pl.multiple_of(place_ref[0] * half, half), half)
        upstream = part_ref[here, :].astype(jnp.float32) + other_ref[...].astype(jnp.float32)
        back_ref[...] = norm_back(stream_ref[here, :], gain_ref[...], upstream).astype(jnp.bfloat16)

    return pl.pallas_call(
        kernel,
        in_specs=[pl.BlockSpec(memory_space=pltpu.SMEM)] + in_vmem(4),
        out_specs=pl.BlockSpec(memory_space=pltpu.VMEM),
        out_shape=jax.ShapeDtypeStruct((half, width), jnp.bfloat16),
        **params(20 * half * width, 12 * half * width),
    )(place, stream, part, other, gain.reshape(1, -1))


def whole_rows(held):
    return in_order(held, shift(held, "mp"), 0) if lax.axis_size("mp") == 2 else held


def per_device(
    resid,
    gain_mlp,
    gain_out,
    w_in,
    w_out,
    a_dino,
    b_dino,
    a_sig,
    b_sig,
    dino_feats,
    sig_feats,
    owner,
):
    n_chips = lax.axis_size("dp")
    n_cores = lax.axis_size("teach")
    width = resid.shape[2]
    rows = resid.shape[0] * resid.shape[1]
    factor = 1.0 / math.sqrt(n_chips * n_cores * rows)
    total_images = owner.shape[0]
    chip = lax.axis_index("dp")
    core = lax.axis_index("teach")

    two = lax.axis_size("mp") == 2
    resid = resid.reshape(rows, width)
    info = jnp.stack([core, chip, lax.axis_index("mp")]).astype(jnp.int32)
    feats = (dino_feats, sig_feats)
    if two:
        peers = [shift(part, "mp") for part in feats]
    ring_r = [shift(resid, "dp", -1)]
    normed, hidden, slope, out_part = mlp_forward(resid, gain_mlp, w_in, w_out)
    if two:
        *peers, out_part = tie(*peers, out_part)
    out_addends = addends_mp(out_part)
    if n_chips > 2:
        ring_r[0], out_part = tie(ring_r[0], out_part)
        ring_r.append(shift(ring_r[0], "dp", -1))
    if two:
        mine, theirs = route_features(info, owner, feats, peers)
        blocks = pair_up(mine, shift(theirs, "teach"))
        *blocks, arrived = tie(*blocks, out_addends[1])
        out_addends = (out_part, arrived)
        targets = [blocks[0]] + [shift(blocks[k], "dp", k) for k in range(1, n_chips)]
    else:
        images = jnp.arange(total_images, dtype=jnp.int32)
        inverse = jnp.sum(jnp.where(owner[None, :] == images[:, None], images[None, :], 0), axis=1)
        feats = [lax.all_gather(part, "mp", axis=2, tiled=True) for part in feats]
        sent = jnp.concatenate(feats, axis=2)
        sent = sent.at[inverse].get(mode="promise_in_bounds", unique_indices=True)
        got = lax.all_to_all(sent, ("dp", "teach"), split_axis=0, concat_axis=1, tiled=True)
        targets = [got.reshape(rows, -1)]

    a_sig_t = a_sig.T
    n_units = b_dino.shape[0]
    stream, summary, act, slope_t, pred_dino, pred_sig = adaptors_forward(
        resid, out_addends, gain_out, a_dino, a_sig_t, b_dino, b_sig
    )
    if n_chips > 2:
        ring_r[1], *_ = tie(ring_r[1], *targets, pred_dino)
    while len(ring_r) < n_chips - 1:
        ring_r.append(shift(ring_r[-1], "dp", -1))
    sig_addends, dino_addends = addends_mp(pred_sig), addends_mp(pred_dino)
    back_sig = loss_gradient(info, sig_addends, targets, b_dino.shape[1], factor)

    n_blocks = n_chips * n_cores
    cols_d, cols_s = slice(0, n_units), slice(n_units, n_units + b_sig.shape[0])
    back_dino, down, part = adaptors_back(
        info, dino_addends, targets, back_sig, (b_dino, b_sig), slope_t, (a_dino, a_sig_t), factor
    )
    ring_r[-1], part = tie(ring_r[-1], part)
    mine_b, theirs_b = gradient_blocks(core, [(back_dino, act, cols_d), (back_sig, act, cols_s)], n_blocks)
    if two:
        half = rows // 2
        place = lax.axis_index("mp").astype(jnp.int32).reshape(1)
        other = shift(lax.dynamic_slice_in_dim(part, (1 - place[0]) * half, half, 0), "mp")
        other, theirs_b = tie(other, theirs_b)
        back = back_rows(place, stream, part, other, gain_out)
    else:
        back = norm_back(stream, gain_out, addends_mp(part)[0].astype(jnp.float32)).astype(jnp.bfloat16)
    down, back = tie(down, back)
    mine_a, theirs_a = gradient_blocks(core, [(summary, down, slice(0, down.shape[1]))], n_blocks)

    def chip_block(sums, i):
        return lax.dynamic_index_in_dim(sums, lax.rem(i + 2 * n_chips, n_chips), 0, keepdims=False)

    def core_sum(mine, theirs):
        got = shift(theirs, "teach")
        return (mine.astype(jnp.float32) + got.astype(jnp.float32)).astype(jnp.bfloat16)

    def block(i):
        return jnp.concatenate([chip_block(chip_b, i), chip_block(chip_a, i)], axis=0)

    chip_b, chip_a = core_sum(mine_b, theirs_b), core_sum(mine_a, theirs_a)
    held = block(chip - 1)
    def add_block(got, step):
        total = got.astype(jnp.float32) + block(chip - 1 - step).astype(jnp.float32)
        return total, total.astype(jnp.bfloat16)

    held_s = [back, shift(back, "dp", -1)]
    held_s[1], held = tie(held_s[1], held)
    for step in range(2, n_chips):
        rows_in, sums_in = tie(shift(held_s[-1], "dp", -1), shift(held, "dp"))
        total, held = add_block(sums_in, step - 1)
        held_s.append(rows_in)
    total, held = add_block(shift(held, "dp"), n_chips - 1)
    total_b, total_a = total[: chip_b.shape[1]], total[chip_b.shape[1] :]
    backs = jnp.concatenate([whole_rows(rows_half) for rows_half in held_s], axis=0)
    depth_d, depth_s = (b.shape[1] // n_blocks for b in (b_dino, b_sig))
    out_a_d, out_a_s = total_a[:, cols_d], total_a[:, cols_s]
    out_b_d, out_b_s = total_b[:depth_d, cols_d].T, total_b[:depth_s, cols_s].T

    *others, _ = tie(*ring_r, held_s[1])
    others = jnp.concatenate(others, axis=0).astype(jnp.float32)
    others = layer_norm(others, gain_mlp).astype(jnp.bfloat16)
    normeds = jnp.concatenate([normed, others], axis=0)
    other_hidden, other_slope = gelu_and_slope(matmul(others, w_in))
    hiddens = jnp.concatenate([hidden, other_hidden], axis=0)
    slopes = jnp.concatenate([slope, other_slope], axis=0)
    back_hidden = (slopes * contract_cols(backs, w_out)).astype(jnp.bfloat16)
    share = width // (n_chips * n_cores)

    def shares(values):
        at = chip * n_cores + core
        own = lax.dynamic_slice_in_dim(values, at * share, share, 1)
        peer = chip * n_cores + (1 - core)
        return own, lax.dynamic_slice_in_dim(values, peer * share, share, 1)

    own_n, peer_n = shares(normeds)
    own_s, peer_s = shares(backs)
    sent_out = contract_rows(hiddens, peer_s).astype(jnp.bfloat16)
    got_out = shift(sent_out, "teach")
    sent_in = contract_rows(peer_n, back_hidden).astype(jnp.bfloat16)
    got_in = shift(sent_in, "teach")
    out_wo = contract_rows(hiddens, own_s) + got_out.astype(jnp.float32)
    out_wi = contract_rows(own_n, back_hidden) + got_in.astype(jnp.float32)
    return out_wi, out_wo, out_a_d, out_b_d, out_a_s, out_b_s


def solution(mesh):
    placed = (
        P(("groups", "dp", "teach"), None, None),
        P(),
        P(),
        P(None, "mp"),
        P("mp", None),
        P(None, "mp"),
        P("mp", None),
        P(None, "mp"),
        P("mp", None),
        P("groups", ("dp", "teach"), "mp"),
        P("groups", ("dp", "teach"), "mp"),
        P("groups"),
    )
    return jax.shard_map(
        per_device,
        mesh=mesh,
        in_specs=placed,
        out_specs=(
            P(("groups", "dp", "teach"), "mp"),
            P(("groups", "mp"), ("dp", "teach")),
            P(("groups", "dp", "teach"), "mp"),
            P(("groups", "mp"), ("dp", "teach")),
            P(("groups", "dp", "teach"), "mp"),
            P(("groups", "mp"), ("dp", "teach")),
        ),
        check_vma=False,
    )
```

```python
import math

import jax
import jax.numpy as jnp
from jax import lax
from jax.experimental import pallas as pl
from jax.experimental.pallas import tpu as pltpu
from jax.sharding import PartitionSpec as P

EPS = 1e-06
ROOT = math.sqrt(2.0 / math.pi)
CUBE = 0.044715


def layer_norm(values, gain):
    center = values - jnp.mean(values, axis=-1, keepdims=True)
    spread = jnp.mean(center * center, axis=-1, keepdims=True)
    return center * lax.rsqrt(spread + EPS) * gain


def norm_back(values, gain, upstream):
    center = values - jnp.mean(values, axis=-1, keepdims=True)
    recip = lax.rsqrt(jnp.mean(center * center, axis=-1, keepdims=True) + EPS)
    unit = center * recip
    scaled = upstream * gain
    return recip * (
        scaled
        - jnp.mean(scaled, axis=-1, keepdims=True)
        - unit * jnp.mean(scaled * unit, axis=-1, keepdims=True)
    )


def gelu_and_slope(values):
    square = values * values
    bend = jnp.tanh(ROOT * values * (1.0 + CUBE * square))
    half = 0.5 * (1.0 + bend)
    slope = half + 0.5 * values * (1.0 - bend * bend) * (ROOT * (1.0 + 3.0 * CUBE * square))
    return (values * half).astype(jnp.bfloat16), slope.astype(jnp.bfloat16)


def tiles(count, step=256):
    return [(at, min(at + step, count)) for at in range(0, count, step)]


def in_vmem(count):
    return [pl.BlockSpec(memory_space=pltpu.VMEM)] * count


def row_dot(left, right):
    return lax.dot_general(
        left, right, (((1,), (1,)), ((), ())), preferred_element_type=jnp.float32
    )


def over_rows(left, right):
    return lax.dot_general(
        left, right, (((0,), (0,)), ((), ())), preferred_element_type=jnp.float32
    )


def params(flops, nbytes, room=8):
    return dict(
        compiler_params=pltpu.CompilerParams(vmem_limit_bytes=room * 1024 * 1024),
        cost_estimate=pl.CostEstimate(flops=flops, bytes_accessed=nbytes, transcendentals=0),
    )


def mlp_forward(resid, gain, w_in, w_out):
    rows, width = resid.shape
    units = w_in.shape[1]
    steps = 2 if units % 256 == 0 else 1
    tile = units // steps

    def kernel(resid_ref, gain_ref, w_in_hbm, w_out_hbm, normed_ref, hid_ref, slope_ref, out_ref, w_in_ref, w_out_ref, in_sem, out_sem):
        def into(at):
            cut = pl.ds(at * tile, tile)
            return pltpu.make_async_copy(w_in_hbm.at[:, cut], w_in_ref.at[:, cut], in_sem.at[at])

        def out_of(at):
            cut = pl.ds(at * tile, tile)
            return pltpu.make_async_copy(w_out_hbm.at[cut, :], w_out_ref.at[cut, :], out_sem.at[at])

        for at in range(steps):
            into(at).start()
        normed_ref[...] = layer_norm(resid_ref[...].astype(jnp.float32), gain_ref[...]).astype(jnp.bfloat16)
        for at in range(steps):
            into(at).wait()
            out_of(at).start()
            for lo, hi in tiles(tile):
                here = slice(at * tile + lo, at * tile + hi)
                hidden, slope = gelu_and_slope(matmul(normed_ref[...], w_in_ref[:, here]))
                hid_ref[:, here] = hidden
                slope_ref[:, here] = slope
        for at in range(steps):
            out_of(at).wait()
        for lo, hi in tiles(width):
            out_ref[:, lo:hi] = matmul(hid_ref[...], w_out_ref[:, lo:hi]).astype(jnp.bfloat16)

    shape = lambda *dims: jax.ShapeDtypeStruct(dims, jnp.bfloat16)
    return pl.pallas_call(
        kernel,
        in_specs=in_vmem(2) + [pl.BlockSpec(memory_space=pltpu.HBM)] * 2,
        out_specs=in_vmem(4),
        out_shape=[shape(rows, width), shape(rows, units), shape(rows, units), shape(rows, width)],
        scratch_shapes=[
            pltpu.VMEM((width, units), jnp.bfloat16),
            pltpu.VMEM((units, width), jnp.bfloat16),
            pltpu.SemaphoreType.DMA((steps,)),
            pltpu.SemaphoreType.DMA((steps,)),
        ],
        **params(4 * rows * width * units, 4 * width * units, 54),
    )(resid, gain, w_in, w_out)


def mlp_hidden(residuals, gain, w_in):
    rows, width = residuals[0].shape
    units = w_in.shape[1]
    count = len(residuals)

    def kernel(gain_ref, w_ref, *refs):
        normed_ref, hid_ref, slope_ref = refs[count:]
        for at, ref in enumerate(refs[:count]):
            here = slice(at * rows, (at + 1) * rows)
            normed_ref[here, :] = layer_norm(ref[...].astype(jnp.float32), gain_ref[...]).astype(jnp.bfloat16)
        for lo, hi in tiles(units):
            for at in range(count):
                here = slice(at * rows, (at + 1) * rows)
                hidden, slope = gelu_and_slope(matmul(normed_ref[here, :], w_ref[:, lo:hi]))
                hid_ref[here, lo:hi] = hidden
                slope_ref[here, lo:hi] = slope

    shape = lambda cols: jax.ShapeDtypeStruct((count * rows, cols), jnp.bfloat16)
    return pl.pallas_call(
        kernel,
        in_specs=in_vmem(2 + count),
        out_specs=in_vmem(3),
        out_shape=[shape(width), shape(units), shape(units)],
        **params(2 * count * rows * width * units, 2 * width * units),
    )(gain, w_in, *residuals)


def chip_blocks(info, mine, theirs):
    n_chips, _, cols = mine[0].shape
    depths = [part.shape[1] for part in mine]
    count = len(mine)

    def kernel(info_ref, *refs):
        for back, out in enumerate(refs[2 * count :]):
            place = lax.rem(info_ref[1] + 2 * n_chips - 1 - back, n_chips)
            top = 0
            for own, other, depth in zip(refs[:count], refs[count : 2 * count], depths):
                value = own[place].astype(jnp.float32) + other[place].astype(jnp.float32)
                out[top : top + depth, :] = value.astype(jnp.bfloat16)
                top += depth

    return pl.pallas_call(
        kernel,
        in_specs=[pl.BlockSpec(memory_space=pltpu.SMEM)] + in_vmem(2 * count),
        out_specs=in_vmem(n_chips),
        out_shape=[jax.ShapeDtypeStruct((sum(depths), cols), jnp.bfloat16)] * n_chips,
        **params(n_chips * sum(depths) * cols, 6 * n_chips * sum(depths) * cols),
    )(info, *mine, *theirs)


def finish_sums(got, block, pieces):
    def kernel(got_ref, block_ref, *refs):
        for (row, depth, col, cols), ref in zip(pieces, refs):
            here = (slice(row, row + depth), slice(col, col + cols))
            ref[...] = got_ref[here].astype(jnp.float32) + block_ref[here].astype(jnp.float32)

    return pl.pallas_call(
        kernel,
        in_specs=in_vmem(2),
        out_specs=in_vmem(len(pieces)),
        out_shape=[jax.ShapeDtypeStruct((depth, cols), jnp.float32) for _, depth, _, cols in pieces],
        **params(got.size, 8 * got.size),
    )(got, block)


def mlp_back(info, halves, w_out, normed_cols, hiddens, slopes, n_chips):
    half, width = halves[0][0].shape
    count = len(halves)
    rows = 2 * half
    units = w_out.shape[0]
    chip_cols = width // n_chips
    share = chip_cols // 2
    flat = [part for pair in halves for part in pair]
    chunk = next(c for c in (512, 256, 128, units) if units % c == 0)
    chunks = units // chunk
    ahead = 2

    def kernel(info_ref, *refs):
        pieces = refs[: 2 * count]
        cols_ref, w_hbm, hid_a, hid_b, slope_a, slope_b, *refs = refs[2 * count :]
        own_in, own_out, their_in, their_out, *refs = refs
        w_ref, hid_ref, slope_ref, backs, back_hidden, back_cols, result, w_sem, slope_sem, hid_sem = refs
        core, chip, place = info_ref[0], info_ref[1], info_ref[2]
        first = hid_a.shape[0]
        spans = ((0, first), (first, count * rows))

        def copies(at):
            cut = pl.ds(at * chunk, chunk)
            parts = [pltpu.make_async_copy(w_hbm.at[cut, :], w_ref.at[cut, :], w_sem.at[at])]
            for which, (source, (top, end)) in enumerate(zip((slope_a, slope_b), spans)):
                here = slope_ref.at[pl.ds(top, end - top), cut]
                parts.append(pltpu.make_async_copy(source.at[:, cut], here, slope_sem.at[which, at]))
            return parts

        def hidden_copies():
            return [
                pltpu.make_async_copy(source, hid_ref.at[pl.ds(top, end - top), :], hid_sem.at[which])
                for which, (source, (top, end)) in enumerate(zip((hid_a, hid_b), spans))
            ]

        for at in range(min(ahead, chunks)):
            for copy in copies(at):
                copy.start()
        for at, ref in enumerate(pieces):
            which = place if at % 2 == 0 else 1 - place
            start = (at // 2) * rows + which * half
            backs[pl.ds(pl.multiple_of(start, half), half), :] = ref[...]
        for j in range(n_chips):

            @pl.when(chip == j)
            def _():
                back_cols[...] = backs[:, j * chip_cols : (j + 1) * chip_cols]

        for at in range(chunks):
            if at + ahead < chunks:
                for copy in copies(at + ahead):
                    copy.start()
            elif at + ahead == chunks or chunks < ahead and at == 0:
                for copy in hidden_copies():
                    copy.start()
            for copy in copies(at):
                copy.wait()
            for left, right in tiles(chunk):
                cut = slice(at * chunk + left, at * chunk + right)
                for image in range(count):
                    here = slice(image * rows, (image + 1) * rows)
                    grown = row_dot(backs[here, :], w_ref[cut, :])
                    back_hidden[here, cut] = (slope_ref[here, cut].astype(jnp.float32) * grown).astype(jnp.bfloat16)

        mine = pl.ds(pl.multiple_of(core * share, share), share)
        theirs = pl.ds(pl.multiple_of((1 - core) * share, share), share)

        def put(value, own, their, cut):
            result[...] = value
            own[:, cut] = result[mine, :]
            their[:, cut] = result[theirs, :].astype(jnp.bfloat16)

        spread = next(c for c in (640, 512, 256, 128, units) if units % c == 0)
        for lo, hi in tiles(units, spread):
            put(over_rows(cols_ref[...], back_hidden[:, lo:hi]), own_in, their_in, slice(lo, hi))
        for copy in hidden_copies():
            copy.wait()
        for lo, hi in tiles(units, spread):
            put(over_rows(back_cols[...], hid_ref[:, lo:hi]), own_out, their_out, slice(lo, hi))

    mine = jax.ShapeDtypeStruct((share, units), jnp.float32)
    theirs = jax.ShapeDtypeStruct((share, units), jnp.bfloat16)
    whole = lambda cols: pltpu.VMEM((count * rows, cols), jnp.bfloat16)
    spread = next(c for c in (640, 512, 256, 128, units) if units % c == 0)
    return pl.pallas_call(
        kernel,
        in_specs=[pl.BlockSpec(memory_space=pltpu.SMEM)]
        + in_vmem(2 * count + 1)
        + [pl.BlockSpec(memory_space=pltpu.HBM)] * 5,
        out_specs=in_vmem(4),
        out_shape=[mine, mine, theirs, theirs],
        scratch_shapes=[
            pltpu.VMEM((units, width), jnp.bfloat16),
            whole(units),
            whole(units),
            whole(width),
            whole(units),
            whole(chip_cols),
            pltpu.VMEM((chip_cols, spread), jnp.float32),
            pltpu.SemaphoreType.DMA((chunks,)),
            pltpu.SemaphoreType.DMA((2, chunks)),
            pltpu.SemaphoreType.DMA((2,)),
        ],
        **params(2 * count * rows * units * (width + 2 * chip_cols), 2 * units * (width + 3 * count * rows), 46),
    )(info, *flat, normed_cols, w_out, *hiddens, *slopes)


def route_features(info, owner, own, peer):
    images, patches, _ = own[0].shape
    n_chips = images // 2
    channels = 2 * sum(part.shape[2] for part in own)

    def kernel(info_ref, owner_ref, own_d, own_s, peer_d, peer_s, mine_ref, theirs_ref):
        core, chip, first = info_ref[0], info_ref[1], info_ref[2] == 0

        def one(image, carry):
            to = owner_ref[image]
            place = lax.rem(to // 2 - chip + n_chips, n_chips)
            pieces = []
            for here, there in ((own_d, peer_d), (own_s, peer_s)):
                a, b = here[image], there[image]
                pieces += [jnp.where(first, a, b), jnp.where(first, b, a)]
            joined = jnp.concatenate(pieces, axis=-1)

            @pl.when(lax.rem(to, 2) == core)
            def _():
                mine_ref[place] = joined

            @pl.when(lax.rem(to, 2) != core)
            def _():
                theirs_ref[place] = joined

            return carry

        lax.fori_loop(0, images, one, 0)

    return pl.pallas_call(
        kernel,
        in_specs=[pl.BlockSpec(memory_space=pltpu.SMEM)] * 2 + in_vmem(4),
        out_specs=in_vmem(2),
        out_shape=[jax.ShapeDtypeStruct((n_chips, patches, channels), jnp.bfloat16)] * 2,
        **params(images * patches * channels, 4 * images * patches * channels),
    )(info, owner, *own, *peer)


def pair_up(mine, theirs):
    n_chips, patches, channels = mine.shape

    def kernel(mine_ref, theirs_ref, *refs):
        for at, ref in enumerate(refs):
            ref[0] = mine_ref[at]
            ref[1] = theirs_ref[at]

    return pl.pallas_call(
        kernel,
        in_specs=in_vmem(2),
        out_specs=in_vmem(n_chips),
        out_shape=[jax.ShapeDtypeStruct((2, patches, channels), jnp.bfloat16)] * n_chips,
        **params(n_chips * patches * channels, 8 * n_chips * patches * channels),
    )(mine, theirs)


def adaptors_forward(resid, addends, gain, a_dino, a_sig, b_dino, b_sig):
    rows, width = resid.shape
    count = len(addends)
    wide, narrow = a_dino.shape[1], a_sig.shape[0]

    def kernel(resid_ref, gain_ref, ad_ref, as_ref, bd_ref, bs_ref, *refs):
        stream = resid_ref[...].astype(jnp.float32)
        added = refs[0][...].astype(jnp.float32)
        for ref in refs[1:count]:
            added = added + ref[...].astype(jnp.float32)
        stream = stream + added
        stream_ref, summary_ref, act_ref, slope_ref, pred_ref = refs[count:]
        stream_ref[...] = stream
        summary_ref[...] = layer_norm(stream, gain_ref[...]).astype(jnp.bfloat16)
        for lo, hi in tiles(narrow):
            act, slope = gelu_and_slope(row_dot(summary_ref[...], as_ref[lo:hi, :]))
            act_ref[:, wide + lo : wide + hi] = act
            slope_ref[:, wide + lo : wide + hi] = slope
        for lo, hi in tiles(bs_ref.shape[1]):
            value = matmul(act_ref[:, wide:], bs_ref[:, lo:hi])
            pred_ref[:, bd_ref.shape[1] + lo : bd_ref.shape[1] + hi] = value.astype(jnp.bfloat16)
        for lo, hi in tiles(wide):
            act, slope = gelu_and_slope(matmul(summary_ref[...], ad_ref[:, lo:hi]))
            act_ref[:, lo:hi] = act
            slope_ref[:, lo:hi] = slope
        for lo, hi in tiles(bd_ref.shape[1]):
            pred_ref[:, lo:hi] = matmul(act_ref[:, :wide], bd_ref[:, lo:hi]).astype(jnp.bfloat16)

    shape = lambda cols, dtype=jnp.bfloat16: jax.ShapeDtypeStruct((rows, cols), dtype)
    work = width * (wide + narrow) + b_dino.size + b_sig.size
    return pl.pallas_call(
        kernel,
        in_specs=in_vmem(6 + count),
        out_specs=in_vmem(5),
        out_shape=[
            shape(width, jnp.float32),
            shape(width),
            shape(wide + narrow),
            shape(wide + narrow),
            shape(b_dino.shape[1] + b_sig.shape[1]),
        ],
        **params(2 * rows * work, 2 * work),
    )(resid, gain, a_dino, a_sig, b_dino, b_sig, *addends)


def loss_rows(info_ref, addends, targets, start, back_ref, factor):
    rows, channels = back_ref.shape
    core, chip = info_ref[0], info_ref[1]
    n_from, patches = len(targets), targets[0].shape[-2]

    def block(here, goal):
        goal = goal.astype(jnp.float32)
        value = addends[0][here, start : start + channels].astype(jnp.float32)
        for ref in addends[1:]:
            value = value + ref[here, start : start + channels].astype(jnp.float32)
        norm_pred = jnp.sum(value * value, axis=-1, keepdims=True) + channels * EPS
        norm_target = jnp.sum(goal * goal, axis=-1, keepdims=True) + channels * EPS
        recip = lax.rsqrt(norm_pred * norm_target)
        cosine = jnp.sum(value * goal, axis=-1, keepdims=True) * recip
        of_pred = factor * (1.0 + channels * (cosine / norm_pred))
        of_target = factor * (1.0 + channels * recip)
        back_ref[here, :] = (value * of_pred - goal * of_target).astype(jnp.bfloat16)

    for at, ref in enumerate(targets):
        if len(ref.shape) == 2:
            for lo, hi in tiles(rows, 32):
                block(slice(lo, hi), ref[lo:hi, start : start + channels])
            continue
        source = lax.rem(chip - at + n_from, n_from)
        for other in range(2):
            place = 2 * source + (1 - core if other else core)
            here = pl.ds(pl.multiple_of(place * patches, patches), patches)
            block(here, ref[other, :, start : start + channels])


def adaptors_back(info, addends, targets, b_weights, slope, a_weights, factor):
    rows = addends[0].shape[0]
    width = a_weights[0].shape[0]
    units = [w.shape[0] for w in b_weights]
    count = len(addends) + len(targets)

    def kernel(info_ref, *refs):
        b_d, b_s, slope_ref, a_d, a_s, back_d, back_s, down_ref, part_ref = refs[count:]
        for start, back in ((0, back_d), (b_d.shape[1], back_s)):
            loss_rows(info_ref, refs[: len(addends)], refs[len(addends) : count], start, back, factor)
        start = 0
        for back, weights in ((back_d, b_d), (back_s, b_s)):
            for lo, hi in tiles(weights.shape[0]):
                grown = row_dot(back[...], weights[lo:hi, :])
                down = slope_ref[:, start + lo : start + hi].astype(jnp.float32) * grown
                down_ref[:, start + lo : start + hi] = down.astype(jnp.bfloat16)
            start += weights.shape[0]
        for lo, hi in tiles(width):
            total = row_dot(down_ref[:, : units[0]], a_d[lo:hi, :])
            total = total + matmul(down_ref[:, units[0] :], a_s[:, lo:hi])
            part_ref[:, lo:hi] = total.astype(jnp.bfloat16)

    work = sum(u * (w.shape[1] + width) for u, w in zip(units, b_weights))
    shape = lambda cols: jax.ShapeDtypeStruct((rows, cols), jnp.bfloat16)
    return pl.pallas_call(
        kernel,
        in_specs=[pl.BlockSpec(memory_space=pltpu.SMEM)] + in_vmem(count + 5),
        out_specs=in_vmem(4),
        out_shape=[*(shape(w.shape[1]) for w in b_weights), shape(sum(units)), shape(width)],
        **params(2 * rows * work, 2 * work, 48),
    )(info, *addends, *targets, *b_weights, slope, *a_weights)


def gradient_blocks(core, pairs, n_blocks):
    rows = pairs[0][0].shape[0]
    depths = [left.shape[1] // n_blocks for left, _, _ in pairs]
    depth = max(depths)
    widths = [cols.stop - cols.start for _, _, cols in pairs]
    count = len(pairs)

    def kernel(core_ref, *refs):
        own = core_ref[0]
        mine_ref, theirs_ref = refs[2 * count :]

        def put(value, at, per, start):
            row = at
            while row < at + value.shape[0]:
                block, inside = row // per, row % per
                stop = min(at + value.shape[0], (block + 1) * per)
                piece = value[row - at : stop - at]
                place = (block // 2, slice(inside, inside + stop - row), slice(start, start + value.shape[1]))

                @pl.when(own == block % 2)
                def _():
                    mine_ref[place] = piece

                @pl.when(own != block % 2)
                def _():
                    theirs_ref[place] = piece

                row = stop

        start = 0
        for at, (per, width) in enumerate(zip(depths, widths)):
            left, right, cols = refs[2 * at], refs[2 * at + 1], pairs[at][2]
            if per < depth:
                blank = jnp.zeros((n_blocks // 2, depth - per, width), jnp.bfloat16)
                mine_ref[:, per:, start : start + width] = blank
                theirs_ref[:, per:, start : start + width] = blank
            for lo, hi in tiles(left.shape[1]):
                value = lax.dot_general(
                    left[:, lo:hi], right[:, cols], (((0,), (0,)), ((), ())), preferred_element_type=jnp.float32
                )
                put(value.astype(jnp.bfloat16), lo, per, start)
            start += width

    work = rows * sum(left.shape[1] * width for (left, _, _), width in zip(pairs, widths))
    return pl.pallas_call(
        kernel,
        in_specs=[pl.BlockSpec(memory_space=pltpu.SMEM)] + in_vmem(2 * count),
        out_specs=in_vmem(2),
        out_shape=[jax.ShapeDtypeStruct((n_blocks // 2, depth, sum(widths)), jnp.bfloat16)] * 2,
        **params(2 * work, 2 * n_blocks * depth * sum(widths)),
    )(core.astype(jnp.int32).reshape(1), *[array for pair in pairs for array in pair[:2]])


def matmul(left, right):
    return jnp.dot(left, right, preferred_element_type=jnp.float32)


def contract_rows(left, right):
    return lax.dot_general(
        left, right, (((0,), (0,)), ((), ())), preferred_element_type=jnp.float32
    )


def contract_cols(left, right):
    return lax.dot_general(
        left, right, (((1,), (1,)), ((), ())), preferred_element_type=jnp.float32
    )


def shift(values, axis, by=1):
    count = lax.axis_size(axis)
    return lax.ppermute(values, axis, [(i, (i + by) % count) for i in range(count)])


def addends_mp(part):
    if lax.axis_size("mp") == 2:
        return (part, shift(part, "mp"))
    return (lax.psum(part, "mp"),)


def in_order(own, other, axis):
    first = lax.axis_index("mp") == 0
    return jnp.concatenate(
        [jnp.where(first, own, other), jnp.where(first, other, own)], axis=axis
    )


def tie(*values):
    return lax.optimization_barrier(values)


def back_rows(place, stream, part, other, gain):
    half, width = other.shape

    def kernel(place_ref, stream_ref, part_ref, other_ref, gain_ref, back_ref):
        here = pl.ds(pl.multiple_of(place_ref[0] * half, half), half)
        upstream = part_ref[here, :].astype(jnp.float32) + other_ref[...].astype(jnp.float32)
        back_ref[...] = norm_back(stream_ref[here, :], gain_ref[...], upstream).astype(jnp.bfloat16)

    return pl.pallas_call(
        kernel,
        in_specs=[pl.BlockSpec(memory_space=pltpu.SMEM)] + in_vmem(4),
        out_specs=pl.BlockSpec(memory_space=pltpu.VMEM),
        out_shape=jax.ShapeDtypeStruct((half, width), jnp.bfloat16),
        **params(20 * half * width, 12 * half * width),
    )(place, stream, part, other, gain)


def per_device(
    resid,
    gain_mlp,
    gain_out,
    w_in,
    w_out,
    a_dino,
    b_dino,
    a_sig,
    b_sig,
    dino_feats,
    sig_feats,
    owner,
):
    n_chips = lax.axis_size("dp")
    n_cores = lax.axis_size("teach")
    width = resid.shape[2]
    rows = resid.shape[0] * resid.shape[1]
    factor = 1.0 / math.sqrt(n_chips * n_cores * rows)
    total_images = owner.shape[0]
    chip = lax.axis_index("dp")
    core = lax.axis_index("teach")

    two = lax.axis_size("mp") == 2
    resid = resid.reshape(rows, width)
    info = jnp.stack([core, chip, lax.axis_index("mp")]).astype(jnp.int32)
    feats = (dino_feats, sig_feats)
    ring_r = [shift(resid, "dp", -1)]
    if two:
        peers = [shift(part, "mp") for part in feats]
    normed, hidden, slope, out_part = mlp_forward(resid, gain_mlp, w_in, w_out)
    if two:
        *peers, ring_r[0], out_part = tie(*peers, ring_r[0], out_part)
    out_addends = addends_mp(out_part)
    if n_chips > 2:
        ring_r.append(shift(ring_r[0], "dp", -1))
    if two:
        mine, theirs = route_features(info, owner, feats, peers)
        blocks = pair_up(mine, shift(theirs, "teach"))
        *blocks, ring_r[-1], arrived = tie(*blocks, ring_r[-1], out_addends[1])
        out_addends = (out_part, arrived)
        targets = [blocks[0]] + [shift(blocks[k], "dp", k) for k in range(1, n_chips)]
    else:
        images = jnp.arange(total_images, dtype=jnp.int32)
        inverse = jnp.sum(jnp.where(owner[None, :] == images[:, None], images[None, :], 0), axis=1)
        feats = [lax.all_gather(part, "mp", axis=2, tiled=True) for part in feats]
        sent = jnp.concatenate(feats, axis=2)
        sent = sent.at[inverse].get(mode="promise_in_bounds", unique_indices=True)
        got = lax.all_to_all(sent, ("dp", "teach"), split_axis=0, concat_axis=1, tiled=True)
        targets = [got.reshape(rows, -1)]

    a_sig_t = a_sig.T
    n_units = b_dino.shape[0]
    stream, summary, act, slope_t, pred = adaptors_forward(
        resid, out_addends, gain_out, a_dino, a_sig_t, b_dino, b_sig
    )
    pred_addends = addends_mp(pred)
    while len(ring_r) < n_chips - 1:
        ring_r[-1], *_ = tie(ring_r[-1], *pred_addends)
        ring_r.append(shift(ring_r[-1], "dp", -1))
    back_dino, back_sig, down, part = adaptors_back(
        info, pred_addends, targets, (b_dino, b_sig), slope_t, (a_dino, a_sig_t), factor
    )

    n_blocks = n_chips * n_cores
    cols_d, cols_s = slice(0, n_units), slice(n_units, n_units + b_sig.shape[0])
    mine_b, theirs_b = gradient_blocks(core, [(back_dino, act, cols_d), (back_sig, act, cols_s)], n_blocks)
    mine_a, theirs_a = gradient_blocks(core, [(summary, down, slice(0, down.shape[1]))], n_blocks)
    if two:
        half = rows // 2
        place = lax.axis_index("mp").astype(jnp.int32).reshape(1)
        other = shift(lax.dynamic_slice_in_dim(part, (1 - place[0]) * half, half, 0), "mp")
        other, theirs_b, theirs_a, ring_r[-1] = tie(other, theirs_b, theirs_a, ring_r[-1])
        back = back_rows(place, stream, part, other, gain_out)
    else:
        back = norm_back(stream, gain_out, addends_mp(part)[0].astype(jnp.float32)).astype(jnp.bfloat16)

    held_s = [back]
    rows_in, got_b, got_a = tie(shift(back, "dp", -1), shift(theirs_b, "teach"), shift(theirs_a, "teach"))
    if two:
        swapped = [shift(back, "mp")]
        swapped[0], rows_in = tie(swapped[0], rows_in)
    held_s.append(rows_in)
    held, *sums = chip_blocks(info, (mine_a, mine_b), (got_a, got_b))

    def columns(values, at, count):
        return lax.dynamic_slice_in_dim(values, at * count, count, 1)

    others = tie(*ring_r, held_s[1])[:-1]
    others, other_hidden, other_slope = mlp_hidden(others, gain_mlp, w_in)
    normeds = jnp.concatenate([normed, others], axis=0)
    normed_cols = columns(normeds, chip, width // n_chips)
    sums_in = shift(held, "dp")
    for step in range(2, n_chips):
        rows_in = shift(held_s[-1], "dp", -1)
        if step == 2:
            rows_in, other_slope = tie(rows_in, other_slope)
        if two:
            last, rows_in = tie(shift(held_s[-1], "mp"), rows_in)
            swapped.append(last)
        if step == n_chips - 1:
            rows_in, sums_in = tie(rows_in, sums_in)
        held_s.append(rows_in)
    hiddens, slopes = (hidden, other_hidden), (slope, other_slope)
    for step in range(1, n_chips - 1):
        held = (sums_in.astype(jnp.float32) + sums[step - 1].astype(jnp.float32)).astype(jnp.bfloat16)
        sums_in = shift(held, "dp")
        if two and step == max(1, n_chips - 3):
            swapped += [shift(part, "mp") for part in held_s[len(swapped) :]]
            halves = list(zip(held_s, swapped))
            outs = mlp_back(info, halves, w_out, normed_cols, hiddens, slopes, n_chips)
            sums_in, own_in, own_out, their_in, their_out = tie(sums_in, *outs)
    if two:
        adds = [(own_in, shift(their_in, "teach")), (own_out, shift(their_out, "teach"))]
    else:
        backs = jnp.concatenate(held_s, axis=0)
        back_hidden = (jnp.concatenate(slopes, axis=0) * contract_cols(backs, w_out)).astype(jnp.bfloat16)
        share = width // n_blocks
        place = chip * n_cores + core
        peer = chip * n_cores + (1 - core)
        all_hidden = jnp.concatenate(hiddens, axis=0)
        sent_out = contract_rows(all_hidden, columns(backs, peer, share)).astype(jnp.bfloat16)
        sent_in = contract_rows(columns(normeds, peer, share), back_hidden).astype(jnp.bfloat16)
        own_out = contract_rows(all_hidden, columns(backs, place, share)).T
        own_in = contract_rows(columns(normeds, place, share), back_hidden)
        adds = [(own_in, shift(sent_in, "teach")), (own_out, shift(sent_out.T, "teach"))]
    depth_a = mine_a.shape[1]
    depth_d, depth_s = (b.shape[1] // n_blocks for b in (b_dino, b_sig))
    narrow = b_sig.shape[0]
    out_wi, out_wo = [own + got.astype(jnp.float32) for own, got in adds]
    sums_in, out_wi, out_wo = tie(sums_in, out_wi, out_wo)
    out_a_d, out_a_s, out_b_d, out_b_s = finish_sums(
        sums_in,
        sums[-1],
        [(0, depth_a, 0, n_units), (0, depth_a, n_units, narrow), (depth_a, depth_d, 0, n_units), (depth_a, depth_s, n_units, narrow)],
    )
    out_wo, out_b_d, out_b_s = out_wo.T, out_b_d.T, out_b_s.T
    return out_wi, out_wo, out_a_d, out_b_d, out_a_s, out_b_s


def solution(mesh):
    placed = (
        P(("groups", "dp", "teach"), None, None),
        P(),
        P(),
        P(None, "mp"),
        P("mp", None),
        P(None, "mp"),
        P("mp", None),
        P(None, "mp"),
        P("mp", None),
        P("groups", ("dp", "teach"), "mp"),
        P("groups", ("dp", "teach"), "mp"),
        P("groups"),
    )
    return jax.shard_map(
        per_device,
        mesh=mesh,
        in_specs=placed,
        out_specs=(
            P(("groups", "dp", "teach"), "mp"),
            P(("groups", "mp"), ("dp", "teach")),
            P(("groups", "dp", "teach"), "mp"),
            P(("groups", "mp"), ("dp", "teach")),
            P(("groups", "dp", "teach"), "mp"),
            P(("groups", "mp"), ("dp", "teach")),
        ),
        check_vma=False,
    )
```

```python
import math

import jax
import jax.numpy as jnp
from jax import lax
from jax.experimental import pallas as pl
from jax.experimental.pallas import tpu as pltpu
from jax.sharding import PartitionSpec as P

EPS = 1e-06
ROOT = math.sqrt(2.0 / math.pi)
CUBE = 0.044715


def layer_norm(values, gain):
    center = values - jnp.mean(values, axis=-1, keepdims=True)
    spread = jnp.mean(center * center, axis=-1, keepdims=True)
    return center * lax.rsqrt(spread + EPS) * gain


def norm_back(values, gain, upstream):
    center = values - jnp.mean(values, axis=-1, keepdims=True)
    recip = lax.rsqrt(jnp.mean(center * center, axis=-1, keepdims=True) + EPS)
    unit = center * recip
    scaled = upstream * gain
    return recip * (
        scaled
        - jnp.mean(scaled, axis=-1, keepdims=True)
        - unit * jnp.mean(scaled * unit, axis=-1, keepdims=True)
    )


def gelu_and_slope(values):
    square = values * values
    bend = jnp.tanh(ROOT * values * (1.0 + CUBE * square))
    half = 0.5 * (1.0 + bend)
    slope = half + 0.5 * values * (1.0 - bend * bend) * (ROOT * (1.0 + 3.0 * CUBE * square))
    return (values * half).astype(jnp.bfloat16), slope.astype(jnp.bfloat16)


def tiles(count, step=256):
    return [(at, min(at + step, count)) for at in range(0, count, step)]


def lanes(at, size):
    return pl.ds(pl.multiple_of(at * size, size), size)


def in_vmem(count):
    return [pl.BlockSpec(memory_space=pltpu.VMEM)] * count


def row_dot(left, right):
    return lax.dot_general(
        left, right, (((1,), (1,)), ((), ())), preferred_element_type=jnp.float32
    )


def over_rows(left, right):
    return lax.dot_general(
        left, right, (((0,), (0,)), ((), ())), preferred_element_type=jnp.float32
    )


def params(flops, nbytes, room=8):
    return dict(
        compiler_params=pltpu.CompilerParams(vmem_limit_bytes=room * 1024 * 1024),
        cost_estimate=pl.CostEstimate(flops=flops, bytes_accessed=nbytes, transcendentals=0),
    )


def mlp_forward(resid, gain, w_in, w_out):
    rows, width = resid.shape
    units = w_in.shape[1]
    steps = 2 if units % 256 == 0 else 1
    tile = units // steps
    step = next(c for c in (256, 128, tile) if tile % c == 0)
    wide = next(c for c in (256, 128, width) if width % c == 0)

    def kernel(resid_ref, gain_ref, w_in_hbm, w_out_hbm, normed_ref, hid_ref, slope_ref, out_ref, w_in_ref, w_out_ref, in_sem, out_sem):
        def into(at):
            cut = pl.ds(at * tile, tile)
            return pltpu.make_async_copy(w_in_hbm.at[:, cut], w_in_ref.at[:, cut], in_sem.at[at])

        def out_of(at):
            cut = pl.ds(at * tile, tile)
            return pltpu.make_async_copy(w_out_hbm.at[cut, :], w_out_ref.at[cut, :], out_sem.at[at])

        for at in range(steps):
            into(at).start()
        normed_ref[...] = layer_norm(resid_ref[...].astype(jnp.float32), gain_ref[...]).astype(jnp.bfloat16)
        for at in range(steps):
            into(at).wait()
            out_of(at).start()
            per = tile // step

            def one(i, carry, at=at):
                here = lanes(at * per + i, step)
                hidden, slope = gelu_and_slope(matmul(normed_ref[...], w_in_ref[:, here]))
                hid_ref[:, here] = hidden
                slope_ref[:, here] = slope
                return carry

            lax.fori_loop(0, per, one, 0)
        for at in range(steps):
            out_of(at).wait()

        def out_tile(i, carry):
            here = lanes(i, wide)
            out_ref[:, here] = matmul(hid_ref[...], w_out_ref[:, here]).astype(jnp.bfloat16)
            return carry

        lax.fori_loop(0, width // wide, out_tile, 0)

    shape = lambda *dims: jax.ShapeDtypeStruct(dims, jnp.bfloat16)
    return pl.pallas_call(
        kernel,
        in_specs=in_vmem(2) + [pl.BlockSpec(memory_space=pltpu.HBM)] * 2,
        out_specs=in_vmem(4),
        out_shape=[shape(rows, width), shape(rows, units), shape(rows, units), shape(rows, width)],
        scratch_shapes=[
            pltpu.VMEM((width, units), jnp.bfloat16),
            pltpu.VMEM((units, width), jnp.bfloat16),
            pltpu.SemaphoreType.DMA((steps,)),
            pltpu.SemaphoreType.DMA((steps,)),
        ],
        **params(4 * rows * width * units, 4 * width * units, 54),
    )(resid, gain, w_in, w_out)


def mlp_hidden(residuals, gain, w_in):
    rows, width = residuals[0].shape
    units = w_in.shape[1]
    step = next(c for c in (256, 128, units) if units % c == 0)
    count = len(residuals)

    def kernel(gain_ref, w_ref, *refs):
        normed_ref, hid_ref, slope_ref = refs[count:]
        for at, ref in enumerate(refs[:count]):
            here = slice(at * rows, (at + 1) * rows)
            normed_ref[here, :] = layer_norm(ref[...].astype(jnp.float32), gain_ref[...]).astype(jnp.bfloat16)
        per = units // step

        def one(at, carry):
            here, cut = lanes(at // per, rows), lanes(lax.rem(at, per), step)
            hidden, slope = gelu_and_slope(matmul(normed_ref[here, :], w_ref[:, cut]))
            hid_ref[here, cut] = hidden
            slope_ref[here, cut] = slope
            return carry

        lax.fori_loop(0, count * per, one, 0)

    shape = lambda cols: jax.ShapeDtypeStruct((count * rows, cols), jnp.bfloat16)
    return pl.pallas_call(
        kernel,
        in_specs=in_vmem(2 + count),
        out_specs=in_vmem(3),
        out_shape=[shape(width), shape(units), shape(units)],
        **params(2 * count * rows * width * units, 2 * width * units),
    )(gain, w_in, *residuals)


def chip_blocks(info, mine, theirs):
    n_chips, _, cols = mine[0].shape
    depths = [part.shape[1] for part in mine]
    count = len(mine)

    def kernel(info_ref, *refs):
        for back, out in enumerate(refs[2 * count :]):
            place = lax.rem(info_ref[1] + 2 * n_chips - 1 - back, n_chips)
            top = 0
            for own, other, depth in zip(refs[:count], refs[count : 2 * count], depths):
                value = own[place].astype(jnp.float32) + other[place].astype(jnp.float32)
                out[top : top + depth, :] = value.astype(jnp.bfloat16)
                top += depth

    return pl.pallas_call(
        kernel,
        in_specs=[pl.BlockSpec(memory_space=pltpu.SMEM)] + in_vmem(2 * count),
        out_specs=in_vmem(n_chips),
        out_shape=[jax.ShapeDtypeStruct((sum(depths), cols), jnp.bfloat16)] * n_chips,
        **params(n_chips * sum(depths) * cols, 6 * n_chips * sum(depths) * cols),
    )(info, *mine, *theirs)


def finish_sums(got, block, pieces):
    def kernel(got_ref, block_ref, *refs):
        for (row, depth, col, cols), ref in zip(pieces, refs):
            here = (slice(row, row + depth), slice(col, col + cols))
            ref[...] = got_ref[here].astype(jnp.float32) + block_ref[here].astype(jnp.float32)

    return pl.pallas_call(
        kernel,
        in_specs=in_vmem(2),
        out_specs=in_vmem(len(pieces)),
        out_shape=[jax.ShapeDtypeStruct((depth, cols), jnp.float32) for _, depth, _, cols in pieces],
        **params(got.size, 8 * got.size),
    )(got, block)


def mlp_back(info, halves, w_out, normed_cols, hiddens, slopes, n_chips):
    half, width = halves[0][0].shape
    count = len(halves)
    rows = 2 * half
    units = w_out.shape[0]
    chip_cols = width // n_chips
    share = chip_cols // 2
    flat = [part for pair in halves for part in pair]
    chunk = next(c for c in (512, 256, 128, units) if units % c == 0)
    chunks = units // chunk
    ahead = 2

    def kernel(info_ref, *refs):
        pieces = refs[: 2 * count]
        cols_ref, w_hbm, hid_a, hid_b, slope_a, slope_b, *refs = refs[2 * count :]
        own_in, own_out, their_in, their_out, *refs = refs
        w_ref, hid_ref, slope_ref, backs, back_hidden, back_cols, result, w_sem, slope_sem, hid_sem = refs
        core, chip, place = info_ref[0], info_ref[1], info_ref[2]
        first = hid_a.shape[0]
        spans = ((0, first), (first, count * rows))

        def copies(at):
            cut = pl.ds(at * chunk, chunk)
            parts = [pltpu.make_async_copy(w_hbm.at[cut, :], w_ref.at[cut, :], w_sem.at[at])]
            for which, (source, (top, end)) in enumerate(zip((slope_a, slope_b), spans)):
                here = slope_ref.at[pl.ds(top, end - top), cut]
                parts.append(pltpu.make_async_copy(source.at[:, cut], here, slope_sem.at[which, at]))
            return parts

        def hidden_copies():
            return [
                pltpu.make_async_copy(source, hid_ref.at[pl.ds(top, end - top), :], hid_sem.at[which])
                for which, (source, (top, end)) in enumerate(zip((hid_a, hid_b), spans))
            ]

        for at in range(min(ahead, chunks)):
            for copy in copies(at):
                copy.start()
        for at, ref in enumerate(pieces):
            which = place if at % 2 == 0 else 1 - place
            start = (at // 2) * rows + which * half
            backs[pl.ds(pl.multiple_of(start, half), half), :] = ref[...]
        for j in range(n_chips):

            @pl.when(chip == j)
            def _():
                back_cols[...] = backs[:, j * chip_cols : (j + 1) * chip_cols]

        for at in range(chunks):
            if at + ahead < chunks:
                for copy in copies(at + ahead):
                    copy.start()
            elif at + ahead == chunks or chunks < ahead and at == 0:
                for copy in hidden_copies():
                    copy.start()
            for copy in copies(at):
                copy.wait()
            for left, right in tiles(chunk):
                cut = slice(at * chunk + left, at * chunk + right)
                for image in range(count):
                    here = slice(image * rows, (image + 1) * rows)
                    grown = row_dot(backs[here, :], w_ref[cut, :])
                    back_hidden[here, cut] = (slope_ref[here, cut].astype(jnp.float32) * grown).astype(jnp.bfloat16)

        mine = pl.ds(pl.multiple_of(core * share, share), share)
        theirs = pl.ds(pl.multiple_of((1 - core) * share, share), share)

        def put(value, own, their, cut):
            result[...] = value
            own[:, cut] = result[mine, :]
            their[:, cut] = result[theirs, :].astype(jnp.bfloat16)

        spread = next(c for c in (640, 512, 256, 128, units) if units % c == 0)
        for lo, hi in tiles(units, spread):
            put(over_rows(cols_ref[...], back_hidden[:, lo:hi]), own_in, their_in, slice(lo, hi))
        for copy in hidden_copies():
            copy.wait()
        for lo, hi in tiles(units, spread):
            put(over_rows(back_cols[...], hid_ref[:, lo:hi]), own_out, their_out, slice(lo, hi))

    mine = jax.ShapeDtypeStruct((share, units), jnp.float32)
    theirs = jax.ShapeDtypeStruct((share, units), jnp.bfloat16)
    whole = lambda cols: pltpu.VMEM((count * rows, cols), jnp.bfloat16)
    spread = next(c for c in (640, 512, 256, 128, units) if units % c == 0)
    return pl.pallas_call(
        kernel,
        in_specs=[pl.BlockSpec(memory_space=pltpu.SMEM)]
        + in_vmem(2 * count + 1)
        + [pl.BlockSpec(memory_space=pltpu.HBM)] * 5,
        out_specs=in_vmem(4),
        out_shape=[mine, mine, theirs, theirs],
        scratch_shapes=[
            pltpu.VMEM((units, width), jnp.bfloat16),
            whole(units),
            whole(units),
            whole(width),
            whole(units),
            whole(chip_cols),
            pltpu.VMEM((chip_cols, spread), jnp.float32),
            pltpu.SemaphoreType.DMA((chunks,)),
            pltpu.SemaphoreType.DMA((2, chunks)),
            pltpu.SemaphoreType.DMA((2,)),
        ],
        **params(2 * count * rows * units * (width + 2 * chip_cols), 2 * units * (width + 3 * count * rows), 46),
    )(info, *flat, normed_cols, w_out, *hiddens, *slopes)


def route_features(info, owner, own, peer):
    images, patches, _ = own[0].shape
    n_chips = images // 2
    channels = 2 * sum(part.shape[2] for part in own)

    def kernel(info_ref, owner_ref, own_d, own_s, peer_d, peer_s, mine_ref, theirs_ref):
        core, chip, first = info_ref[0], info_ref[1], info_ref[2] == 0

        def one(image, carry):
            to = owner_ref[image]
            place = lax.rem(to // 2 - chip + n_chips, n_chips)
            pieces = []
            for here, there in ((own_d, peer_d), (own_s, peer_s)):
                a, b = here[image], there[image]
                pieces += [jnp.where(first, a, b), jnp.where(first, b, a)]
            joined = jnp.concatenate(pieces, axis=-1)

            @pl.when(lax.rem(to, 2) == core)
            def _():
                mine_ref[place] = joined

            @pl.when(lax.rem(to, 2) != core)
            def _():
                theirs_ref[place] = joined

            return carry

        lax.fori_loop(0, images, one, 0)

    return pl.pallas_call(
        kernel,
        in_specs=[pl.BlockSpec(memory_space=pltpu.SMEM)] * 2 + in_vmem(4),
        out_specs=in_vmem(2),
        out_shape=[jax.ShapeDtypeStruct((n_chips, patches, channels), jnp.bfloat16)] * 2,
        **params(images * patches * channels, 4 * images * patches * channels),
    )(info, owner, *own, *peer)


def pair_up(mine, theirs):
    n_chips, patches, channels = mine.shape

    def kernel(mine_ref, theirs_ref, *refs):
        for at, ref in enumerate(refs):
            ref[0] = mine_ref[at]
            ref[1] = theirs_ref[at]

    return pl.pallas_call(
        kernel,
        in_specs=in_vmem(2),
        out_specs=in_vmem(n_chips),
        out_shape=[jax.ShapeDtypeStruct((2, patches, channels), jnp.bfloat16)] * n_chips,
        **params(n_chips * patches * channels, 8 * n_chips * patches * channels),
    )(mine, theirs)


def adaptors_forward(resid, addends, gain, a_dino, a_sig, b_dino, b_sig):
    rows, width = resid.shape
    count = len(addends)
    wide, narrow = a_dino.shape[1], a_sig.shape[0]

    def kernel(resid_ref, gain_ref, ad_ref, as_ref, bd_ref, bs_ref, *refs):
        stream = resid_ref[...].astype(jnp.float32)
        added = refs[0][...].astype(jnp.float32)
        for ref in refs[1:count]:
            added = added + ref[...].astype(jnp.float32)
        stream = stream + added
        stream_ref, summary_ref, act_ref, slope_ref, pred_ref = refs[count:]
        stream_ref[...] = stream
        summary_ref[...] = layer_norm(stream, gain_ref[...]).astype(jnp.bfloat16)
        for lo, hi in tiles(narrow):
            act, slope = gelu_and_slope(row_dot(summary_ref[...], as_ref[lo:hi, :]))
            act_ref[:, wide + lo : wide + hi] = act
            slope_ref[:, wide + lo : wide + hi] = slope
        for lo, hi in tiles(bs_ref.shape[1]):
            value = matmul(act_ref[:, wide:], bs_ref[:, lo:hi])
            pred_ref[:, bd_ref.shape[1] + lo : bd_ref.shape[1] + hi] = value.astype(jnp.bfloat16)
        for lo, hi in tiles(wide):
            act, slope = gelu_and_slope(matmul(summary_ref[...], ad_ref[:, lo:hi]))
            act_ref[:, lo:hi] = act
            slope_ref[:, lo:hi] = slope
        for lo, hi in tiles(bd_ref.shape[1]):
            pred_ref[:, lo:hi] = matmul(act_ref[:, :wide], bd_ref[:, lo:hi]).astype(jnp.bfloat16)

    shape = lambda cols, dtype=jnp.bfloat16: jax.ShapeDtypeStruct((rows, cols), dtype)
    work = width * (wide + narrow) + b_dino.size + b_sig.size
    return pl.pallas_call(
        kernel,
        in_specs=in_vmem(6 + count),
        out_specs=in_vmem(5),
        out_shape=[
            shape(width, jnp.float32),
            shape(width),
            shape(wide + narrow),
            shape(wide + narrow),
            shape(b_dino.shape[1] + b_sig.shape[1]),
        ],
        **params(2 * rows * work, 2 * work),
    )(resid, gain, a_dino, a_sig, b_dino, b_sig, *addends)


def loss_rows(info_ref, addends, targets, start, back_ref, factor):
    rows, channels = back_ref.shape
    core, chip = info_ref[0], info_ref[1]
    n_from, patches = len(targets), targets[0].shape[-2]

    def block(here, goal):
        goal = goal.astype(jnp.float32)
        value = addends[0][here, start : start + channels].astype(jnp.float32)
        for ref in addends[1:]:
            value = value + ref[here, start : start + channels].astype(jnp.float32)
        norm_pred = jnp.sum(value * value, axis=-1, keepdims=True) + channels * EPS
        norm_target = jnp.sum(goal * goal, axis=-1, keepdims=True) + channels * EPS
        recip = lax.rsqrt(norm_pred * norm_target)
        cosine = jnp.sum(value * goal, axis=-1, keepdims=True) * recip
        of_pred = factor * (1.0 + channels * (cosine / norm_pred))
        of_target = factor * (1.0 + channels * recip)
        back_ref[here, :] = (value * of_pred - goal * of_target).astype(jnp.bfloat16)

    for at, ref in enumerate(targets):
        if len(ref.shape) == 2:
            for lo, hi in tiles(rows, 32):
                block(slice(lo, hi), ref[lo:hi, start : start + channels])
            continue
        source = lax.rem(chip - at + n_from, n_from)
        for other in range(2):
            place = 2 * source + (1 - core if other else core)
            here = pl.ds(pl.multiple_of(place * patches, patches), patches)
            block(here, ref[other, :, start : start + channels])


def adaptors_back(info, addends, targets, b_weights, slope, a_weights, factor):
    rows = addends[0].shape[0]
    width = a_weights[0].shape[0]
    units = [w.shape[0] for w in b_weights]
    count = len(addends) + len(targets)

    def kernel(info_ref, *refs):
        b_d, b_s, slope_ref, a_d, a_s, back_d, back_s, down_ref, part_ref = refs[count:]
        for start, back in ((0, back_d), (b_d.shape[1], back_s)):
            loss_rows(info_ref, refs[: len(addends)], refs[len(addends) : count], start, back, factor)
        start = 0
        for back, weights in ((back_d, b_d), (back_s, b_s)):
            for lo, hi in tiles(weights.shape[0]):
                grown = row_dot(back[...], weights[lo:hi, :])
                down = slope_ref[:, start + lo : start + hi].astype(jnp.float32) * grown
                down_ref[:, start + lo : start + hi] = down.astype(jnp.bfloat16)
            start += weights.shape[0]
        for lo, hi in tiles(width):
            total = row_dot(down_ref[:, : units[0]], a_d[lo:hi, :])
            total = total + matmul(down_ref[:, units[0] :], a_s[:, lo:hi])
            part_ref[:, lo:hi] = total.astype(jnp.bfloat16)

    work = sum(u * (w.shape[1] + width) for u, w in zip(units, b_weights))
    shape = lambda cols: jax.ShapeDtypeStruct((rows, cols), jnp.bfloat16)
    return pl.pallas_call(
        kernel,
        in_specs=[pl.BlockSpec(memory_space=pltpu.SMEM)] + in_vmem(count + 5),
        out_specs=in_vmem(4),
        out_shape=[*(shape(w.shape[1]) for w in b_weights), shape(sum(units)), shape(width)],
        **params(2 * rows * work, 2 * work, 48),
    )(info, *addends, *targets, *b_weights, slope, *a_weights)


def gradient_blocks(core, pairs, n_blocks):
    rows = pairs[0][0].shape[0]
    depths = [left.shape[1] // n_blocks for left, _, _ in pairs]
    depth = max(depths)
    widths = [cols.stop - cols.start for _, _, cols in pairs]
    count = len(pairs)

    def kernel(core_ref, *refs):
        own = core_ref[0]
        mine_ref, theirs_ref = refs[2 * count :]

        def put(value, at, per, start):
            row = at
            while row < at + value.shape[0]:
                block, inside = row // per, row % per
                stop = min(at + value.shape[0], (block + 1) * per)
                piece = value[row - at : stop - at]
                place = (block // 2, slice(inside, inside + stop - row), slice(start, start + value.shape[1]))

                @pl.when(own == block % 2)
                def _():
                    mine_ref[place] = piece

                @pl.when(own != block % 2)
                def _():
                    theirs_ref[place] = piece

                row = stop

        start = 0
        for at, (per, width) in enumerate(zip(depths, widths)):
            left, right, cols = refs[2 * at], refs[2 * at + 1], pairs[at][2]
            if per < depth:
                blank = jnp.zeros((n_blocks // 2, depth - per, width), jnp.bfloat16)
                mine_ref[:, per:, start : start + width] = blank
                theirs_ref[:, per:, start : start + width] = blank
            for lo, hi in tiles(left.shape[1]):
                value = lax.dot_general(
                    left[:, lo:hi], right[:, cols], (((0,), (0,)), ((), ())), preferred_element_type=jnp.float32
                )
                put(value.astype(jnp.bfloat16), lo, per, start)
            start += width

    work = rows * sum(left.shape[1] * width for (left, _, _), width in zip(pairs, widths))
    return pl.pallas_call(
        kernel,
        in_specs=[pl.BlockSpec(memory_space=pltpu.SMEM)] + in_vmem(2 * count),
        out_specs=in_vmem(2),
        out_shape=[jax.ShapeDtypeStruct((n_blocks // 2, depth, sum(widths)), jnp.bfloat16)] * 2,
        **params(2 * work, 2 * n_blocks * depth * sum(widths)),
    )(core.astype(jnp.int32).reshape(1), *[array for pair in pairs for array in pair[:2]])


def matmul(left, right):
    return jnp.dot(left, right, preferred_element_type=jnp.float32)


def contract_rows(left, right):
    return lax.dot_general(
        left, right, (((0,), (0,)), ((), ())), preferred_element_type=jnp.float32
    )


def contract_cols(left, right):
    return lax.dot_general(
        left, right, (((1,), (1,)), ((), ())), preferred_element_type=jnp.float32
    )


def shift(values, axis, by=1):
    count = lax.axis_size(axis)
    return lax.ppermute(values, axis, [(i, (i + by) % count) for i in range(count)])


def addends_mp(part):
    if lax.axis_size("mp") == 2:
        return (part, shift(part, "mp"))
    return (lax.psum(part, "mp"),)


def in_order(own, other, axis):
    first = lax.axis_index("mp") == 0
    return jnp.concatenate(
        [jnp.where(first, own, other), jnp.where(first, other, own)], axis=axis
    )


def tie(*values):
    return lax.optimization_barrier(values)


def back_rows(place, stream, part, other, gain):
    half, width = other.shape

    def kernel(place_ref, stream_ref, part_ref, other_ref, gain_ref, back_ref):
        here = pl.ds(pl.multiple_of(place_ref[0] * half, half), half)
        upstream = part_ref[here, :].astype(jnp.float32) + other_ref[...].astype(jnp.float32)
        back_ref[...] = norm_back(stream_ref[here, :], gain_ref[...], upstream).astype(jnp.bfloat16)

    return pl.pallas_call(
        kernel,
        in_specs=[pl.BlockSpec(memory_space=pltpu.SMEM)] + in_vmem(4),
        out_specs=pl.BlockSpec(memory_space=pltpu.VMEM),
        out_shape=jax.ShapeDtypeStruct((half, width), jnp.bfloat16),
        **params(20 * half * width, 12 * half * width),
    )(place, stream, part, other, gain)


def per_device(
    resid,
    gain_mlp,
    gain_out,
    w_in,
    w_out,
    a_dino,
    b_dino,
    a_sig,
    b_sig,
    dino_feats,
    sig_feats,
    owner,
):
    n_chips = lax.axis_size("dp")
    n_cores = lax.axis_size("teach")
    width = resid.shape[2]
    rows = resid.shape[0] * resid.shape[1]
    factor = 1.0 / math.sqrt(n_chips * n_cores * rows)
    total_images = owner.shape[0]
    chip = lax.axis_index("dp")
    core = lax.axis_index("teach")

    two = lax.axis_size("mp") == 2
    resid = resid.reshape(rows, width)
    info = jnp.stack([core, chip, lax.axis_index("mp")]).astype(jnp.int32)
    feats = (dino_feats, sig_feats)
    ring_r = [shift(resid, "dp", -1)]
    if two:
        peers = [shift(part, "mp") for part in feats]
    normed, hidden, slope, out_part = mlp_forward(resid, gain_mlp, w_in, w_out)
    if two:
        *peers, ring_r[0], out_part = tie(*peers, ring_r[0], out_part)
    out_addends = addends_mp(out_part)
    if n_chips > 2:
        ring_r.append(shift(ring_r[0], "dp", -1))
    if two:
        mine, theirs = route_features(info, owner, feats, peers)
        blocks = pair_up(mine, shift(theirs, "teach"))
        *blocks, ring_r[-1], arrived = tie(*blocks, ring_r[-1], out_addends[1])
        out_addends = (out_part, arrived)
        targets = [blocks[0]] + [shift(blocks[k], "dp", k) for k in range(1, n_chips)]
    else:
        images = jnp.arange(total_images, dtype=jnp.int32)
        inverse = jnp.sum(jnp.where(owner[None, :] == images[:, None], images[None, :], 0), axis=1)
        feats = [lax.all_gather(part, "mp", axis=2, tiled=True) for part in feats]
        sent = jnp.concatenate(feats, axis=2)
        sent = sent.at[inverse].get(mode="promise_in_bounds", unique_indices=True)
        got = lax.all_to_all(sent, ("dp", "teach"), split_axis=0, concat_axis=1, tiled=True)
        targets = [got.reshape(rows, -1)]

    a_sig_t = a_sig.T
    n_units = b_dino.shape[0]
    stream, summary, act, slope_t, pred = adaptors_forward(
        resid, out_addends, gain_out, a_dino, a_sig_t, b_dino, b_sig
    )
    pred_addends = addends_mp(pred)
    while len(ring_r) < n_chips - 1:
        ring_r[-1], *_ = tie(ring_r[-1], *pred_addends)
        ring_r.append(shift(ring_r[-1], "dp", -1))
    back_dino, back_sig, down, part = adaptors_back(
        info, pred_addends, targets, (b_dino, b_sig), slope_t, (a_dino, a_sig_t), factor
    )

    n_blocks = n_chips * n_cores
    cols_d, cols_s = slice(0, n_units), slice(n_units, n_units + b_sig.shape[0])
    mine_b, theirs_b = gradient_blocks(core, [(back_dino, act, cols_d), (back_sig, act, cols_s)], n_blocks)
    mine_a, theirs_a = gradient_blocks(core, [(summary, down, slice(0, down.shape[1]))], n_blocks)
    if two:
        half = rows // 2
        place = lax.axis_index("mp").astype(jnp.int32).reshape(1)
        other = shift(lax.dynamic_slice_in_dim(part, (1 - place[0]) * half, half, 0), "mp")
        other, theirs_b, theirs_a, ring_r[-1] = tie(other, theirs_b, theirs_a, ring_r[-1])
        back = back_rows(place, stream, part, other, gain_out)
    else:
        back = norm_back(stream, gain_out, addends_mp(part)[0].astype(jnp.float32)).astype(jnp.bfloat16)

    held_s = [back]
    rows_in, got_b, got_a = tie(shift(back, "dp", -1), shift(theirs_b, "teach"), shift(theirs_a, "teach"))
    if two:
        swapped = [shift(back, "mp")]
        swapped[0], rows_in = tie(swapped[0], rows_in)
    held_s.append(rows_in)
    held, *sums = chip_blocks(info, (mine_a, mine_b), (got_a, got_b))

    def columns(values, at, count):
        return lax.dynamic_slice_in_dim(values, at * count, count, 1)

    others = tie(*ring_r, held_s[1])[:-1]
    others, other_hidden, other_slope = mlp_hidden(others, gain_mlp, w_in)
    normeds = jnp.concatenate([normed, others], axis=0)
    normed_cols = columns(normeds, chip, width // n_chips)
    sums_in = shift(held, "dp")
    for step in range(2, n_chips):
        rows_in = shift(held_s[-1], "dp", -1)
        if step == 2:
            rows_in, other_slope = tie(rows_in, other_slope)
        if two:
            last, rows_in = tie(shift(held_s[-1], "mp"), rows_in)
            swapped.append(last)
        if step == n_chips - 1:
            rows_in, sums_in = tie(rows_in, sums_in)
        held_s.append(rows_in)
    hiddens, slopes = (hidden, other_hidden), (slope, other_slope)
    for step in range(1, n_chips - 1):
        held = (sums_in.astype(jnp.float32) + sums[step - 1].astype(jnp.float32)).astype(jnp.bfloat16)
        sums_in = shift(held, "dp")
        if two and step == max(1, n_chips - 3):
            swapped += [shift(part, "mp") for part in held_s[len(swapped) :]]
            halves = list(zip(held_s, swapped))
            outs = mlp_back(info, halves, w_out, normed_cols, hiddens, slopes, n_chips)
            sums_in, own_in, own_out, their_in, their_out = tie(sums_in, *outs)
    if two:
        adds = [(own_in, shift(their_in, "teach")), (own_out, shift(their_out, "teach"))]
    else:
        backs = jnp.concatenate(held_s, axis=0)
        back_hidden = (jnp.concatenate(slopes, axis=0) * contract_cols(backs, w_out)).astype(jnp.bfloat16)
        share = width // n_blocks
        place = chip * n_cores + core
        peer = chip * n_cores + (1 - core)
        all_hidden = jnp.concatenate(hiddens, axis=0)
        sent_out = contract_rows(all_hidden, columns(backs, peer, share)).astype(jnp.bfloat16)
        sent_in = contract_rows(columns(normeds, peer, share), back_hidden).astype(jnp.bfloat16)
        own_out = contract_rows(all_hidden, columns(backs, place, share)).T
        own_in = contract_rows(columns(normeds, place, share), back_hidden)
        adds = [(own_in, shift(sent_in, "teach")), (own_out, shift(sent_out.T, "teach"))]
    depth_a = mine_a.shape[1]
    depth_d, depth_s = (b.shape[1] // n_blocks for b in (b_dino, b_sig))
    narrow = b_sig.shape[0]
    out_wi, out_wo = [own + got.astype(jnp.float32) for own, got in adds]
    sums_in, out_wi, out_wo = tie(sums_in, out_wi, out_wo)
    out_a_d, out_a_s, out_b_d, out_b_s = finish_sums(
        sums_in,
        sums[-1],
        [(0, depth_a, 0, n_units), (0, depth_a, n_units, narrow), (depth_a, depth_d, 0, n_units), (depth_a, depth_s, n_units, narrow)],
    )
    out_wo, out_b_d, out_b_s = out_wo.T, out_b_d.T, out_b_s.T
    return out_wi, out_wo, out_a_d, out_b_d, out_a_s, out_b_s


def solution(mesh):
    placed = (
        P(("groups", "dp", "teach"), None, None),
        P(),
        P(),
        P(None, "mp"),
        P("mp", None),
        P(None, "mp"),
        P("mp", None),
        P(None, "mp"),
        P("mp", None),
        P("groups", ("dp", "teach"), "mp"),
        P("groups", ("dp", "teach"), "mp"),
        P("groups"),
    )
    return jax.shard_map(
        per_device,
        mesh=mesh,
        in_specs=placed,
        out_specs=(
            P(("groups", "dp", "teach"), "mp"),
            P(("groups", "mp"), ("dp", "teach")),
            P(("groups", "dp", "teach"), "mp"),
            P(("groups", "mp"), ("dp", "teach")),
            P(("groups", "dp", "teach"), "mp"),
            P(("groups", "mp"), ("dp", "teach")),
        ),
        check_vma=False,
    )
```

```python
import math

import jax
import jax.numpy as jnp
from jax import lax
from jax.experimental import pallas as pl
from jax.experimental.pallas import tpu as pltpu
from jax.sharding import PartitionSpec as P

EPS = 1e-06
ROOT = math.sqrt(2.0 / math.pi)
CUBE = 0.044715


def layer_norm(values, gain):
    center = values - jnp.mean(values, axis=-1, keepdims=True)
    spread = jnp.mean(center * center, axis=-1, keepdims=True)
    return center * lax.rsqrt(spread + EPS) * gain


def norm_back(values, gain, upstream):
    center = values - jnp.mean(values, axis=-1, keepdims=True)
    recip = lax.rsqrt(jnp.mean(center * center, axis=-1, keepdims=True) + EPS)
    unit = center * recip
    scaled = upstream * gain
    return recip * (
        scaled
        - jnp.mean(scaled, axis=-1, keepdims=True)
        - unit * jnp.mean(scaled * unit, axis=-1, keepdims=True)
    )


def gelu_and_slope(values):
    square = values * values
    bend = jnp.tanh(ROOT * values * (1.0 + CUBE * square))
    half = 0.5 * (1.0 + bend)
    slope = half + 0.5 * values * (1.0 - bend * bend) * (ROOT * (1.0 + 3.0 * CUBE * square))
    return (values * half).astype(jnp.bfloat16), slope.astype(jnp.bfloat16)


def tiles(count, step=256):
    return [(at, min(at + step, count)) for at in range(0, count, step)]


def lanes(at, size):
    return pl.ds(pl.multiple_of(at * size, size), size)


def in_vmem(count):
    return [pl.BlockSpec(memory_space=pltpu.VMEM)] * count


def row_dot(left, right):
    return lax.dot_general(
        left, right, (((1,), (1,)), ((), ())), preferred_element_type=jnp.float32
    )


def over_rows(left, right):
    return lax.dot_general(
        left, right, (((0,), (0,)), ((), ())), preferred_element_type=jnp.float32
    )


def params(flops, nbytes, room=8):
    return dict(
        compiler_params=pltpu.CompilerParams(vmem_limit_bytes=room * 1024 * 1024),
        cost_estimate=pl.CostEstimate(flops=flops, bytes_accessed=nbytes, transcendentals=0),
    )


def mlp_forward(resid, gain, w_in, w_out):
    rows, width = resid.shape
    units = w_in.shape[1]
    steps = 2 if units % 256 == 0 else 1
    tile = units // steps
    step = next(c for c in (256, 128, tile) if tile % c == 0)
    wide = next(c for c in (256, 128, width) if width % c == 0)

    def kernel(resid_ref, gain_ref, w_in_hbm, w_out_hbm, normed_ref, hid_ref, slope_ref, out_ref, w_in_ref, w_out_ref, in_sem, out_sem):
        def into(at):
            cut = pl.ds(at * tile, tile)
            return pltpu.make_async_copy(w_in_hbm.at[:, cut], w_in_ref.at[:, cut], in_sem.at[at])

        def out_of(at):
            cut = pl.ds(at * tile, tile)
            return pltpu.make_async_copy(w_out_hbm.at[cut, :], w_out_ref.at[cut, :], out_sem.at[at])

        for at in range(steps):
            into(at).start()
        normed_ref[...] = layer_norm(resid_ref[...].astype(jnp.float32), gain_ref[...]).astype(jnp.bfloat16)
        for at in range(steps):
            into(at).wait()
            out_of(at).start()
            per = tile // step

            def one(i, carry, at=at):
                here = lanes(at * per + i, step)
                hidden, slope = gelu_and_slope(matmul(normed_ref[...], w_in_ref[:, here]))
                hid_ref[:, here] = hidden
                slope_ref[:, here] = slope
                return carry

            lax.fori_loop(0, per, one, 0)
        for at in range(steps):
            out_of(at).wait()

        def out_tile(i, carry):
            here = lanes(i, wide)
            out_ref[:, here] = matmul(hid_ref[...], w_out_ref[:, here]).astype(jnp.bfloat16)
            return carry

        lax.fori_loop(0, width // wide, out_tile, 0)

    shape = lambda *dims: jax.ShapeDtypeStruct(dims, jnp.bfloat16)
    return pl.pallas_call(
        kernel,
        in_specs=in_vmem(2) + [pl.BlockSpec(memory_space=pltpu.HBM)] * 2,
        out_specs=in_vmem(4),
        out_shape=[shape(rows, width), shape(rows, units), shape(rows, units), shape(rows, width)],
        scratch_shapes=[
            pltpu.VMEM((width, units), jnp.bfloat16),
            pltpu.VMEM((units, width), jnp.bfloat16),
            pltpu.SemaphoreType.DMA((steps,)),
            pltpu.SemaphoreType.DMA((steps,)),
        ],
        **params(4 * rows * width * units, 4 * width * units, 54),
    )(resid, gain, w_in, w_out)


def mlp_hidden(residuals, gain, w_in):
    rows, width = residuals[0].shape
    units = w_in.shape[1]
    step = next(c for c in (256, 128, units) if units % c == 0)
    count = len(residuals)

    def kernel(gain_ref, w_ref, *refs):
        normed_ref, hid_ref, slope_ref = refs[count:]
        for at, ref in enumerate(refs[:count]):
            here = slice(at * rows, (at + 1) * rows)
            normed_ref[here, :] = layer_norm(ref[...].astype(jnp.float32), gain_ref[...]).astype(jnp.bfloat16)
        per = units // step

        def one(at, carry):
            here, cut = lanes(at // per, rows), lanes(lax.rem(at, per), step)
            hidden, slope = gelu_and_slope(matmul(normed_ref[here, :], w_ref[:, cut]))
            hid_ref[here, cut] = hidden
            slope_ref[here, cut] = slope
            return carry

        lax.fori_loop(0, count * per, one, 0)

    shape = lambda cols: jax.ShapeDtypeStruct((count * rows, cols), jnp.bfloat16)
    return pl.pallas_call(
        kernel,
        in_specs=in_vmem(2 + count),
        out_specs=in_vmem(3),
        out_shape=[shape(width), shape(units), shape(units)],
        **params(2 * count * rows * width * units, 2 * width * units),
    )(gain, w_in, *residuals)


def chip_blocks(info, mine, theirs):
    n_chips, _, cols = mine[0].shape
    depths = [part.shape[1] for part in mine]
    count = len(mine)

    def kernel(info_ref, *refs):
        for back, out in enumerate(refs[2 * count :]):
            place = lax.rem(info_ref[1] + 2 * n_chips - 1 - back, n_chips)
            top = 0
            for own, other, depth in zip(refs[:count], refs[count : 2 * count], depths):
                value = own[place].astype(jnp.float32) + other[place].astype(jnp.float32)
                out[top : top + depth, :] = value.astype(jnp.bfloat16)
                top += depth

    return pl.pallas_call(
        kernel,
        in_specs=[pl.BlockSpec(memory_space=pltpu.SMEM)] + in_vmem(2 * count),
        out_specs=in_vmem(n_chips),
        out_shape=[jax.ShapeDtypeStruct((sum(depths), cols), jnp.bfloat16)] * n_chips,
        **params(n_chips * sum(depths) * cols, 6 * n_chips * sum(depths) * cols),
    )(info, *mine, *theirs)


def finish_sums(got, block, pieces):
    def kernel(got_ref, block_ref, *refs):
        for (row, depth, col, cols), ref in zip(pieces, refs):
            here = (slice(row, row + depth), slice(col, col + cols))
            ref[...] = got_ref[here].astype(jnp.float32) + block_ref[here].astype(jnp.float32)

    return pl.pallas_call(
        kernel,
        in_specs=in_vmem(2),
        out_specs=in_vmem(len(pieces)),
        out_shape=[jax.ShapeDtypeStruct((depth, cols), jnp.float32) for _, depth, _, cols in pieces],
        **params(got.size, 8 * got.size),
    )(got, block)


def mlp_back(info, halves, w_out, normed_cols, hiddens, slopes, n_chips):
    half, width = halves[0][0].shape
    count = len(halves)
    rows = 2 * half
    units = w_out.shape[0]
    chip_cols = width // n_chips
    share = chip_cols // 2
    flat = [part for pair in halves for part in pair]
    chunk = next(c for c in (512, 256, 128, units) if units % c == 0)
    chunks = units // chunk
    ahead = 2

    def kernel(info_ref, *refs):
        pieces = refs[: 2 * count]
        cols_ref, w_hbm, hid_a, hid_b, slope_a, slope_b, *refs = refs[2 * count :]
        own_in, own_out, their_in, their_out, *refs = refs
        w_ref, hid_ref, slope_ref, backs, back_hidden, back_cols, result, w_sem, slope_sem, hid_sem = refs
        core, chip, place = info_ref[0], info_ref[1], info_ref[2]
        first = hid_a.shape[0]
        spans = ((0, first), (first, count * rows))

        def copies(at):
            cut = pl.ds(at * chunk, chunk)
            parts = [pltpu.make_async_copy(w_hbm.at[cut, :], w_ref.at[cut, :], w_sem.at[at])]
            for which, (source, (top, end)) in enumerate(zip((slope_a, slope_b), spans)):
                here = slope_ref.at[pl.ds(top, end - top), cut]
                parts.append(pltpu.make_async_copy(source.at[:, cut], here, slope_sem.at[which, at]))
            return parts

        def hidden_copies():
            return [
                pltpu.make_async_copy(source, hid_ref.at[pl.ds(top, end - top), :], hid_sem.at[which])
                for which, (source, (top, end)) in enumerate(zip((hid_a, hid_b), spans))
            ]

        for at in range(min(ahead, chunks)):
            for copy in copies(at):
                copy.start()
        for at, ref in enumerate(pieces):
            which = place if at % 2 == 0 else 1 - place
            start = (at // 2) * rows + which * half
            backs[pl.ds(pl.multiple_of(start, half), half), :] = ref[...]
        for j in range(n_chips):

            @pl.when(chip == j)
            def _():
                back_cols[...] = backs[:, j * chip_cols : (j + 1) * chip_cols]

        for at in range(chunks):
            if at + ahead < chunks:
                for copy in copies(at + ahead):
                    copy.start()
            elif at + ahead == chunks or chunks < ahead and at == 0:
                for copy in hidden_copies():
                    copy.start()
            for copy in copies(at):
                copy.wait()
            for left, right in tiles(chunk):
                cut = slice(at * chunk + left, at * chunk + right)
                for image in range(count):
                    here = slice(image * rows, (image + 1) * rows)
                    grown = row_dot(backs[here, :], w_ref[cut, :])
                    back_hidden[here, cut] = (slope_ref[here, cut].astype(jnp.float32) * grown).astype(jnp.bfloat16)

        mine = pl.ds(pl.multiple_of(core * share, share), share)
        theirs = pl.ds(pl.multiple_of((1 - core) * share, share), share)

        def put(value, own, their, cut):
            result[...] = value
            own[:, cut] = result[mine, :]
            their[:, cut] = result[theirs, :].astype(jnp.bfloat16)

        spread = next(c for c in (640, 512, 256, 128, units) if units % c == 0)
        for lo, hi in tiles(units, spread):
            put(over_rows(cols_ref[...], back_hidden[:, lo:hi]), own_in, their_in, slice(lo, hi))
        for copy in hidden_copies():
            copy.wait()
        for lo, hi in tiles(units, spread):
            put(over_rows(back_cols[...], hid_ref[:, lo:hi]), own_out, their_out, slice(lo, hi))

    mine = jax.ShapeDtypeStruct((share, units), jnp.float32)
    theirs = jax.ShapeDtypeStruct((share, units), jnp.bfloat16)
    whole = lambda cols: pltpu.VMEM((count * rows, cols), jnp.bfloat16)
    spread = next(c for c in (640, 512, 256, 128, units) if units % c == 0)
    return pl.pallas_call(
        kernel,
        in_specs=[pl.BlockSpec(memory_space=pltpu.SMEM)]
        + in_vmem(2 * count + 1)
        + [pl.BlockSpec(memory_space=pltpu.HBM)] * 5,
        out_specs=in_vmem(4),
        out_shape=[mine, mine, theirs, theirs],
        scratch_shapes=[
            pltpu.VMEM((units, width), jnp.bfloat16),
            whole(units),
            whole(units),
            whole(width),
            whole(units),
            whole(chip_cols),
            pltpu.VMEM((chip_cols, spread), jnp.float32),
            pltpu.SemaphoreType.DMA((chunks,)),
            pltpu.SemaphoreType.DMA((2, chunks)),
            pltpu.SemaphoreType.DMA((2,)),
        ],
        **params(2 * count * rows * units * (width + 2 * chip_cols), 2 * units * (width + 3 * count * rows), 46),
    )(info, *flat, normed_cols, w_out, *hiddens, *slopes)


def route_features(info, owner, own, peer):
    images, patches, _ = own[0].shape
    n_chips = images // 2
    channels = 2 * sum(part.shape[2] for part in own)

    def kernel(info_ref, owner_ref, own_d, own_s, peer_d, peer_s, mine_ref, theirs_ref):
        core, chip, first = info_ref[0], info_ref[1], info_ref[2] == 0

        def one(image, carry):
            to = owner_ref[image]
            place = lax.rem(to // 2 - chip + n_chips, n_chips)
            pieces = []
            for here, there in ((own_d, peer_d), (own_s, peer_s)):
                a, b = here[image], there[image]
                pieces += [jnp.where(first, a, b), jnp.where(first, b, a)]
            joined = jnp.concatenate(pieces, axis=-1)

            @pl.when(lax.rem(to, 2) == core)
            def _():
                mine_ref[place] = joined

            @pl.when(lax.rem(to, 2) != core)
            def _():
                theirs_ref[place] = joined

            return carry

        lax.fori_loop(0, images, one, 0)

    return pl.pallas_call(
        kernel,
        in_specs=[pl.BlockSpec(memory_space=pltpu.SMEM)] * 2 + in_vmem(4),
        out_specs=in_vmem(2),
        out_shape=[jax.ShapeDtypeStruct((n_chips, patches, channels), jnp.bfloat16)] * 2,
        **params(images * patches * channels, 4 * images * patches * channels),
    )(info, owner, *own, *peer)


def pair_up(mine, theirs):
    n_chips, patches, channels = mine.shape

    def kernel(mine_ref, theirs_ref, *refs):
        for at, ref in enumerate(refs):
            ref[0] = mine_ref[at]
            ref[1] = theirs_ref[at]

    return pl.pallas_call(
        kernel,
        in_specs=in_vmem(2),
        out_specs=in_vmem(n_chips),
        out_shape=[jax.ShapeDtypeStruct((2, patches, channels), jnp.bfloat16)] * n_chips,
        **params(n_chips * patches * channels, 8 * n_chips * patches * channels),
    )(mine, theirs)


def adaptors_forward(resid, addends, gain, a_dino, a_sig, b_dino, b_sig):
    rows, width = resid.shape
    count = len(addends)
    wide, narrow = a_dino.shape[1], a_sig.shape[0]

    def kernel(resid_ref, gain_ref, ad_ref, as_ref, bd_ref, bs_ref, *refs):
        stream = resid_ref[...].astype(jnp.float32)
        added = refs[0][...].astype(jnp.float32)
        for ref in refs[1:count]:
            added = added + ref[...].astype(jnp.float32)
        stream = stream + added
        stream_ref, summary_ref, act_ref, slope_ref, pred_ref = refs[count:]
        stream_ref[...] = stream
        summary_ref[...] = layer_norm(stream, gain_ref[...]).astype(jnp.bfloat16)
        for lo, hi in tiles(narrow):
            act, slope = gelu_and_slope(row_dot(summary_ref[...], as_ref[lo:hi, :]))
            act_ref[:, wide + lo : wide + hi] = act
            slope_ref[:, wide + lo : wide + hi] = slope
        for lo, hi in tiles(bs_ref.shape[1]):
            value = matmul(act_ref[:, wide:], bs_ref[:, lo:hi])
            pred_ref[:, bd_ref.shape[1] + lo : bd_ref.shape[1] + hi] = value.astype(jnp.bfloat16)
        for lo, hi in tiles(wide):
            act, slope = gelu_and_slope(matmul(summary_ref[...], ad_ref[:, lo:hi]))
            act_ref[:, lo:hi] = act
            slope_ref[:, lo:hi] = slope
        for lo, hi in tiles(bd_ref.shape[1]):
            pred_ref[:, lo:hi] = matmul(act_ref[:, :wide], bd_ref[:, lo:hi]).astype(jnp.bfloat16)

    shape = lambda cols, dtype=jnp.bfloat16: jax.ShapeDtypeStruct((rows, cols), dtype)
    work = width * (wide + narrow) + b_dino.size + b_sig.size
    return pl.pallas_call(
        kernel,
        in_specs=in_vmem(6 + count),
        out_specs=in_vmem(5),
        out_shape=[
            shape(width, jnp.float32),
            shape(width),
            shape(wide + narrow),
            shape(wide + narrow),
            shape(b_dino.shape[1] + b_sig.shape[1]),
        ],
        **params(2 * rows * work, 2 * work),
    )(resid, gain, a_dino, a_sig, b_dino, b_sig, *addends)


def loss_rows(info_ref, addends, targets, start, back_ref, factor):
    rows, channels = back_ref.shape
    core, chip = info_ref[0], info_ref[1]
    n_from, patches = len(targets), targets[0].shape[-2]

    def block(here, goal):
        goal = goal.astype(jnp.float32)
        value = addends[0][here, start : start + channels].astype(jnp.float32)
        for ref in addends[1:]:
            value = value + ref[here, start : start + channels].astype(jnp.float32)
        norm_pred = jnp.sum(value * value, axis=-1, keepdims=True) + channels * EPS
        norm_target = jnp.sum(goal * goal, axis=-1, keepdims=True) + channels * EPS
        recip = lax.rsqrt(norm_pred * norm_target)
        cosine = jnp.sum(value * goal, axis=-1, keepdims=True) * recip
        of_pred = factor * (1.0 + channels * (cosine / norm_pred))
        of_target = factor * (1.0 + channels * recip)
        back_ref[here, :] = (value * of_pred - goal * of_target).astype(jnp.bfloat16)

    for at, ref in enumerate(targets):
        if len(ref.shape) == 2:
            for lo, hi in tiles(rows, 32):
                block(slice(lo, hi), ref[lo:hi, start : start + channels])
            continue
        source = lax.rem(chip - at + n_from, n_from)
        for other in range(2):
            place = 2 * source + (1 - core if other else core)
            here = pl.ds(pl.multiple_of(place * patches, patches), patches)
            block(here, ref[other, :, start : start + channels])


def adaptors_back(info, addends, targets, b_weights, slope, a_weights, factor):
    rows = addends[0].shape[0]
    width = a_weights[0].shape[0]
    units = [w.shape[0] for w in b_weights]
    count = len(addends) + len(targets)

    def kernel(info_ref, *refs):
        b_d, b_s, slope_ref, a_d, a_s, back_d, back_s, down_ref, part_ref = refs[count:]
        for start, back in ((0, back_d), (b_d.shape[1], back_s)):
            loss_rows(info_ref, refs[: len(addends)], refs[len(addends) : count], start, back, factor)
        start = 0
        for back, weights in ((back_d, b_d), (back_s, b_s)):
            for lo, hi in tiles(weights.shape[0]):
                grown = row_dot(back[...], weights[lo:hi, :])
                down = slope_ref[:, start + lo : start + hi].astype(jnp.float32) * grown
                down_ref[:, start + lo : start + hi] = down.astype(jnp.bfloat16)
            start += weights.shape[0]
        for lo, hi in tiles(width):
            total = row_dot(down_ref[:, : units[0]], a_d[lo:hi, :])
            total = total + matmul(down_ref[:, units[0] :], a_s[:, lo:hi])
            part_ref[:, lo:hi] = total.astype(jnp.bfloat16)

    work = sum(u * (w.shape[1] + width) for u, w in zip(units, b_weights))
    shape = lambda cols: jax.ShapeDtypeStruct((rows, cols), jnp.bfloat16)
    return pl.pallas_call(
        kernel,
        in_specs=[pl.BlockSpec(memory_space=pltpu.SMEM)] + in_vmem(count + 5),
        out_specs=in_vmem(4),
        out_shape=[*(shape(w.shape[1]) for w in b_weights), shape(sum(units)), shape(width)],
        **params(2 * rows * work, 2 * work, 48),
    )(info, *addends, *targets, *b_weights, slope, *a_weights)


def gradient_blocks(core, pairs, n_blocks):
    rows = pairs[0][0].shape[0]
    depths = [left.shape[1] // n_blocks for left, _, _ in pairs]
    depth = max(depths)
    widths = [cols.stop - cols.start for _, _, cols in pairs]
    count = len(pairs)

    def kernel(core_ref, *refs):
        own = core_ref[0]
        mine_ref, theirs_ref = refs[2 * count :]

        def put(value, at, per, start):
            row = at
            while row < at + value.shape[0]:
                block, inside = row // per, row % per
                stop = min(at + value.shape[0], (block + 1) * per)
                piece = value[row - at : stop - at]
                place = (block // 2, slice(inside, inside + stop - row), slice(start, start + value.shape[1]))

                @pl.when(own == block % 2)
                def _():
                    mine_ref[place] = piece

                @pl.when(own != block % 2)
                def _():
                    theirs_ref[place] = piece

                row = stop

        start = 0
        for at, (per, width) in enumerate(zip(depths, widths)):
            left, right, cols = refs[2 * at], refs[2 * at + 1], pairs[at][2]
            if per < depth:
                blank = jnp.zeros((n_blocks // 2, depth - per, width), jnp.bfloat16)
                mine_ref[:, per:, start : start + width] = blank
                theirs_ref[:, per:, start : start + width] = blank
            for lo, hi in tiles(left.shape[1]):
                value = lax.dot_general(
                    left[:, lo:hi], right[:, cols], (((0,), (0,)), ((), ())), preferred_element_type=jnp.float32
                )
                put(value.astype(jnp.bfloat16), lo, per, start)
            start += width

    work = rows * sum(left.shape[1] * width for (left, _, _), width in zip(pairs, widths))
    return pl.pallas_call(
        kernel,
        in_specs=[pl.BlockSpec(memory_space=pltpu.SMEM)] + in_vmem(2 * count),
        out_specs=in_vmem(2),
        out_shape=[jax.ShapeDtypeStruct((n_blocks // 2, depth, sum(widths)), jnp.bfloat16)] * 2,
        **params(2 * work, 2 * n_blocks * depth * sum(widths)),
    )(core.astype(jnp.int32).reshape(1), *[array for pair in pairs for array in pair[:2]])


def matmul(left, right):
    return jnp.dot(left, right, preferred_element_type=jnp.float32)


def contract_rows(left, right):
    return lax.dot_general(
        left, right, (((0,), (0,)), ((), ())), preferred_element_type=jnp.float32
    )


def contract_cols(left, right):
    return lax.dot_general(
        left, right, (((1,), (1,)), ((), ())), preferred_element_type=jnp.float32
    )


def shift(values, axis, by=1):
    count = lax.axis_size(axis)
    return lax.ppermute(values, axis, [(i, (i + by) % count) for i in range(count)])


def addends_mp(part):
    if lax.axis_size("mp") == 2:
        return (part, shift(part, "mp"))
    return (lax.psum(part, "mp"),)


def in_order(own, other, axis):
    first = lax.axis_index("mp") == 0
    return jnp.concatenate(
        [jnp.where(first, own, other), jnp.where(first, other, own)], axis=axis
    )


def tie(*values):
    return lax.optimization_barrier(values)


def back_rows(place, stream, part, other, gain):
    half, width = other.shape

    def kernel(place_ref, stream_ref, part_ref, other_ref, gain_ref, back_ref):
        here = pl.ds(pl.multiple_of(place_ref[0] * half, half), half)
        upstream = part_ref[here, :].astype(jnp.float32) + other_ref[...].astype(jnp.float32)
        back_ref[...] = norm_back(stream_ref[here, :], gain_ref[...], upstream).astype(jnp.bfloat16)

    return pl.pallas_call(
        kernel,
        in_specs=[pl.BlockSpec(memory_space=pltpu.SMEM)] + in_vmem(4),
        out_specs=pl.BlockSpec(memory_space=pltpu.VMEM),
        out_shape=jax.ShapeDtypeStruct((half, width), jnp.bfloat16),
        **params(20 * half * width, 12 * half * width),
    )(place, stream, part, other, gain)


def per_device(
    resid,
    gain_mlp,
    gain_out,
    w_in,
    w_out,
    a_dino,
    b_dino,
    a_sig,
    b_sig,
    dino_feats,
    sig_feats,
    owner,
):
    n_chips = lax.axis_size("dp")
    n_cores = lax.axis_size("teach")
    width = resid.shape[2]
    rows = resid.shape[0] * resid.shape[1]
    factor = 1.0 / math.sqrt(n_chips * n_cores * rows)
    total_images = owner.shape[0]
    chip = lax.axis_index("dp")
    core = lax.axis_index("teach")

    two = lax.axis_size("mp") == 2
    resid = resid.reshape(rows, width)
    info = jnp.stack([core, chip, lax.axis_index("mp")]).astype(jnp.int32)
    feats = (dino_feats, sig_feats)
    ring_r = [shift(resid, "dp", -1)]
    if two:
        peers = [shift(part, "mp") for part in feats]
    normed, hidden, slope, out_part = mlp_forward(resid, gain_mlp, w_in, w_out)
    if two:
        *peers, ring_r[0], out_part = tie(*peers, ring_r[0], out_part)
    out_addends = addends_mp(out_part)
    if n_chips > 2:
        ring_r.append(shift(ring_r[0], "dp", -1))
    if two:
        mine, theirs = route_features(info, owner, feats, peers)
        blocks = pair_up(mine, shift(theirs, "teach"))
        *blocks, ring_r[-1], arrived = tie(*blocks, ring_r[-1], out_addends[1])
        out_addends = (out_part, arrived)
        targets = [blocks[0]] + [shift(blocks[k], "dp", k) for k in range(1, n_chips)]
    else:
        images = jnp.arange(total_images, dtype=jnp.int32)
        inverse = jnp.sum(jnp.where(owner[None, :] == images[:, None], images[None, :], 0), axis=1)
        feats = [lax.all_gather(part, "mp", axis=2, tiled=True) for part in feats]
        sent = jnp.concatenate(feats, axis=2)
        sent = sent.at[inverse].get(mode="promise_in_bounds", unique_indices=True)
        got = lax.all_to_all(sent, ("dp", "teach"), split_axis=0, concat_axis=1, tiled=True)
        targets = [got.reshape(rows, -1)]

    a_sig_t = a_sig.T
    n_units = b_dino.shape[0]
    stream, summary, act, slope_t, pred = adaptors_forward(
        resid, out_addends, gain_out, a_dino, a_sig_t, b_dino, b_sig
    )
    pred_addends = addends_mp(pred)
    while len(ring_r) < n_chips - 1:
        ring_r[-1], *_ = tie(ring_r[-1], *pred_addends)
        ring_r.append(shift(ring_r[-1], "dp", -1))
    back_dino, back_sig, down, part = adaptors_back(
        info, pred_addends, targets, (b_dino, b_sig), slope_t, (a_dino, a_sig_t), factor
    )

    n_blocks = n_chips * n_cores
    cols_d, cols_s = slice(0, n_units), slice(n_units, n_units + b_sig.shape[0])
    mine_b, theirs_b = gradient_blocks(core, [(back_dino, act, cols_d), (back_sig, act, cols_s)], n_blocks)
    mine_a, theirs_a = gradient_blocks(core, [(summary, down, slice(0, down.shape[1]))], n_blocks)
    if two:
        half = rows // 2
        place = lax.axis_index("mp").astype(jnp.int32).reshape(1)
        other = shift(lax.dynamic_slice_in_dim(part, (1 - place[0]) * half, half, 0), "mp")
        other, theirs_b, theirs_a, ring_r[-1] = tie(other, theirs_b, theirs_a, ring_r[-1])
        back = back_rows(place, stream, part, other, gain_out)
    else:
        back = norm_back(stream, gain_out, addends_mp(part)[0].astype(jnp.float32)).astype(jnp.bfloat16)

    held_s = [back]
    rows_in = shift(back, "dp", -1)
    got_b, got_a = shift(theirs_b, "teach"), shift(theirs_a, "teach")
    held, *sums = chip_blocks(info, (mine_a, mine_b), (got_a, got_b))
    if two:
        swapped = [shift(back, "mp")]
        swapped[0], rows_in, held = tie(swapped[0], rows_in, held)
    held_s.append(rows_in)

    def columns(values, at, count):
        return lax.dynamic_slice_in_dim(values, at * count, count, 1)

    others = tie(*ring_r, held_s[1])[:-1]
    others, other_hidden, other_slope = mlp_hidden(others, gain_mlp, w_in)
    normeds = jnp.concatenate([normed, others], axis=0)
    normed_cols = columns(normeds, chip, width // n_chips)
    sums_in = shift(held, "dp")
    for step in range(2, n_chips):
        rows_in = shift(held_s[-1], "dp", -1)
        if step == 2:
            rows_in, other_slope = tie(rows_in, other_slope)
        if two:
            last, rows_in = tie(shift(held_s[-1], "mp"), rows_in)
            swapped.append(last)
        if step == n_chips - 1:
            rows_in, sums_in = tie(rows_in, sums_in)
        held_s.append(rows_in)
    hiddens, slopes = (hidden, other_hidden), (slope, other_slope)
    for step in range(1, n_chips - 1):
        held = (sums_in.astype(jnp.float32) + sums[step - 1].astype(jnp.float32)).astype(jnp.bfloat16)
        sums_in = shift(held, "dp")
        if two and step == max(1, n_chips - 3):
            swapped += [shift(part, "mp") for part in held_s[len(swapped) :]]
            halves = list(zip(held_s, swapped))
            outs = mlp_back(info, halves, w_out, normed_cols, hiddens, slopes, n_chips)
            sums_in, own_in, own_out, their_in, their_out = tie(sums_in, *outs)
    if two:
        adds = [(own_in, shift(their_in, "teach")), (own_out, shift(their_out, "teach"))]
    else:
        backs = jnp.concatenate(held_s, axis=0)
        back_hidden = (jnp.concatenate(slopes, axis=0) * contract_cols(backs, w_out)).astype(jnp.bfloat16)
        share = width // n_blocks
        place = chip * n_cores + core
        peer = chip * n_cores + (1 - core)
        all_hidden = jnp.concatenate(hiddens, axis=0)
        sent_out = contract_rows(all_hidden, columns(backs, peer, share)).astype(jnp.bfloat16)
        sent_in = contract_rows(columns(normeds, peer, share), back_hidden).astype(jnp.bfloat16)
        own_out = contract_rows(all_hidden, columns(backs, place, share)).T
        own_in = contract_rows(columns(normeds, place, share), back_hidden)
        adds = [(own_in, shift(sent_in, "teach")), (own_out, shift(sent_out.T, "teach"))]
    depth_a = mine_a.shape[1]
    depth_d, depth_s = (b.shape[1] // n_blocks for b in (b_dino, b_sig))
    narrow = b_sig.shape[0]
    out_wi, out_wo = [own + got.astype(jnp.float32) for own, got in adds]
    sums_in, out_wi, out_wo = tie(sums_in, out_wi, out_wo)
    out_a_d, out_a_s, out_b_d, out_b_s = finish_sums(
        sums_in,
        sums[-1],
        [(0, depth_a, 0, n_units), (0, depth_a, n_units, narrow), (depth_a, depth_d, 0, n_units), (depth_a, depth_s, n_units, narrow)],
    )
    out_wo, out_b_d, out_b_s = out_wo.T, out_b_d.T, out_b_s.T
    return out_wi, out_wo, out_a_d, out_b_d, out_a_s, out_b_s


def solution(mesh):
    placed = (
        P(("groups", "dp", "teach"), None, None),
        P(),
        P(),
        P(None, "mp"),
        P("mp", None),
        P(None, "mp"),
        P("mp", None),
        P(None, "mp"),
        P("mp", None),
        P("groups", ("dp", "teach"), "mp"),
        P("groups", ("dp", "teach"), "mp"),
        P("groups"),
    )
    return jax.shard_map(
        per_device,
        mesh=mesh,
        in_specs=placed,
        out_specs=(
            P(("groups", "dp", "teach"), "mp"),
            P(("groups", "mp"), ("dp", "teach")),
            P(("groups", "dp", "teach"), "mp"),
            P(("groups", "mp"), ("dp", "teach")),
            P(("groups", "dp", "teach"), "mp"),
            P(("groups", "mp"), ("dp", "teach")),
        ),
        check_vma=False,
    )
```
